128 devices in a mesh: row: 16 (over y, z_hi, core), col: 8 (over x, z_lo).
Axes of the slice: x: 4, y: 4, z: 4 (z_hi: 2, z_lo: 2; z = z_hi * 2 + z_lo), core: 2. Of those that a mesh axis runs over, the one named last changes fastest.
Arguments:
- pair: bfloat16 [640, 640, 128], P('row', 'col'), may hold values from -6 to 6
- pair_mask: int32 [640, 640], P('row', 'col'), may hold values 0 or 1
- norm_gain: float32 [128], replicated, may hold values from 0.1 to 1.9
- norm_bias: float32 [128], replicated, may hold values from -3 to 3
- proj_weight: bfloat16 [128, 256], replicated, may hold values from -0.5 to 0.5
- gate_weight: bfloat16 [128, 256], replicated, may hold values from -0.5 to 0.5
- out_gain: float32 [128], replicated, may hold values from 0.1 to 1.9
- out_bias: float32 [128], replicated, may hold values from -3 to 3
- out_weight: bfloat16 [128, 128], replicated, may hold values from -0.5 to 0.5
- out_gate_weight: bfloat16 [128, 128], replicated, may hold values from -0.5 to 0.5
Outputs:
- update: bfloat16 [640, 640, 128], P('row', 'col')
The draws below stay inside these ranges and needn't reach their ends.
All inputs are finite; a program needn't handle non-finite values. No bound on the sum of `pair_mask` on one device may be relied on, other than what follows from the above.
Results may differ from the reference program's by a relative error of at most 0.015.
Values may be sent and summed in bfloat16 or wider, within the bound.
A program may use at most 128 MiB of HBM per device.

```python
import jax
import jax.numpy as jnp
from jax import lax

D = 128
HID = 128
N = 640
N_COL = 8


def plant(array, own_key, low, high):
    index_at = [jax.random.randint(jax.random.fold_in(own_key, axis), (), 0, length) for axis, length in enumerate(array.shape)]
    widest = array.shape.index(max(array.shape))
    beside = index_at[:widest] + [(index_at[widest] + 1) % array.shape[widest]] + index_at[widest + 1:]
    return array.at[tuple(index_at)].set(low).at[tuple(beside)].set(high)


def shard_levels(own_key, extent, shards, low, top_value):
    loudness = 1.0
    for dim, shards_of in shards:
        draws = jax.random.uniform(jax.random.fold_in(jax.random.fold_in(own_key, 6), dim), (shards_of,), jnp.float32, low / len(shards), top_value / len(shards))
        loudness = loudness * jnp.repeat(jnp.exp(draws), extent[dim] // shards_of).reshape((-1,) + (1,) * (len(extent) - 1 - dim))
    return loudness


def normal_values(rng, shape, deviation, limit, split=(), dtype=jnp.bfloat16):
    drawn = jax.random.normal(rng, shape, jnp.float32) * deviation
    if len(split) > 0:
        drawn = shard_levels(rng, shape, split, -0.22, 0.18) * drawn
    return jnp.clip(drawn, min=-limit, max=limit).astype(dtype)


def setup_inputs(seed: int = 0) -> dict:
    arg_keys = jax.random.split(jax.random.key(seed), 11)
    return {
        "pair": normal_values(arg_keys[0], (N, N, D), 1.0, 6.0, ((0, 16), (1, 8))),
        "pair_mask": plant((jax.random.randint(arg_keys[1], (N, N), 0, 8) < 7).astype(jnp.int32), jax.random.fold_in(arg_keys[1], 1), 0, 1),
        "norm_gain": jnp.clip(1.0 + 0.18 * jax.random.normal(arg_keys[2], (D,), jnp.float32), 0.1, 1.9),
        "norm_bias": normal_values(arg_keys[3], (D,), 0.5, 3.0, (), jnp.float32),
        "proj_weight": normal_values(arg_keys[4], (D, 2 * HID), D ** -0.5, 0.5),
        "gate_weight": normal_values(arg_keys[5], (D, 2 * HID), D ** -0.5, 0.5),
        "out_gain": jnp.clip(1.0 + 0.18 * jax.random.normal(arg_keys[6], (HID,), jnp.float32), 0.1, 1.9),
        "out_bias": normal_values(arg_keys[7], (HID,), 0.5, 3.0, (), jnp.float32),
        "out_weight": normal_values(arg_keys[8], (HID, D), HID ** -0.5, 0.5),
        "out_gate_weight": normal_values(arg_keys[9], (D, D), D ** -0.5, 0.5),
    }


def layer_norm(values, gain, bias):
    mean = lax.optimization_barrier(jnp.mean(values, axis=-1, keepdims=True))
    centred = values - mean
    var = lax.optimization_barrier(jnp.mean(centred * centred, axis=-1, keepdims=True))
    return centred * lax.rsqrt(var + 1e-05) * gain + bias

def channel_block(operands):
    left_block, right_block = operands
    width = N // N_COL
    left_parts = jnp.moveaxis(left_block.reshape(16, N, N_COL, width), 2, 0)
    right_parts = jnp.moveaxis(right_block.reshape(16, N, N_COL, width), 2, 0)

    def add_block(total, pieces):
        left_piece, right_piece = pieces
        partial_value = jnp.einsum('cik,cjk->cij', left_piece.astype(jnp.float32), right_piece.astype(jnp.float32), precision=lax.Precision.HIGHEST)
        rounded = lax.optimization_barrier(partial_value.astype(jnp.bfloat16))
        return (total + rounded.astype(jnp.float32), None)
    total, unused = lax.scan(add_block, jnp.zeros((16, N, N), jnp.float32), (left_parts, right_parts))
    return total

def reference(pair, pair_mask, norm_gain, norm_bias, proj_weight, gate_weight, out_gain, out_bias, out_weight, out_gate_weight):
    normed = layer_norm(pair.astype(jnp.float32), norm_gain, norm_bias).astype(jnp.bfloat16)
    proj = jnp.dot(normed, proj_weight, preferred_element_type=jnp.float32)
    gate = jnp.dot(normed, gate_weight, preferred_element_type=jnp.float32)
    packed = (proj * jax.nn.sigmoid(gate) * pair_mask[..., None].astype(jnp.float32)).astype(jnp.bfloat16)
    left = jnp.moveaxis(packed[..., :HID], 2, 0).reshape(HID // 16, 16, N, N)
    right = jnp.moveaxis(packed[..., HID:], 2, 0).reshape(HID // 16, 16, N, N)
    blocks = lax.map(channel_block, (left, right))
    combined = jnp.moveaxis(blocks.reshape(HID, N, N), 0, 2)
    finished = layer_norm(combined, out_gain, out_bias).astype(jnp.bfloat16)
    projected = jnp.dot(finished, out_weight, preferred_element_type=jnp.float32)
    gating = jax.nn.sigmoid(jnp.dot(normed, out_gate_weight, preferred_element_type=jnp.float32))
    return (projected * gating).astype(jnp.bfloat16)
```

```python
import functools

import jax
import jax.numpy as jnp
from jax import lax
from jax.experimental import pallas as pl
from jax.experimental.pallas import tpu as pltpu
from jax.sharding import PartitionSpec as P

MESH = pl.DeviceIdType.MESH
F32, BF16 = jnp.float32, jnp.bfloat16
NT = (((1,), (1,)), ((), ()))
CHIPS = 64
ROWS = 112
BACK = 32


def device(x, y, z, core):
    return (y * 4 + (z // 2) * 2 + core, x * 2 + z % 2)


def chip_index(x, y, z):
    return (y * 2 + z // 2) * 8 + x * 2 + z % 2


def kernel(
    pair, mask, norm_gain, norm_bias, proj_w, gate_w, out_gain, out_bias, out_w, out_gate_w,
    out,
    normed, masked, gating, weights, wide, packed, arrived, left, right, swap, combined, back, returned, finished,
    sibling_send, sibling_recv, send, recv, back_send, back_recv, local,
):
    r, c = lax.axis_index("row"), lax.axis_index("col")
    x, y, z, core = c // 2, r // 4, ((r // 2) % 2) * 2 + c % 2, r % 2
    me = chip_index(x, y, z)

    def shifted(step):
        return (x + step // 16) % 4, (y + (step // 4) % 4) % 4, (z + step % 4) % 4

    barrier = pltpu.get_barrier_semaphore()

    def greet(step, carry):
        pl.semaphore_signal(
            barrier, inc=1, device_id=device(*shifted(step // 2), (core + step % 2) % 2), device_id_type=MESH
        )
        return carry

    lax.fori_loop(1, 2 * CHIPS, greet, 0)

    swap[0:128, 0:128] = jnp.zeros((128, 128), BF16)
    swap[0:40, 0:80] = mask[...].astype(F32).astype(BF16)
    mask_t = jnp.transpose(swap[0:128, 0:128].astype(F32))[0:80, :].astype(BF16)
    gain, bias = norm_gain[...], norm_bias[...]

    def norm_row(i, carry):
        values = pair[i].astype(F32)
        mean = jnp.mean(values, axis=-1, keepdims=True)
        centred = values - mean
        var = jnp.mean(centred * centred, axis=-1, keepdims=True)
        n = (centred * lax.rsqrt(var + 1e-05) * gain + bias).astype(BF16)
        normed[i] = n
        pick = (lax.broadcasted_iota(jnp.int32, (128, 128), 0) == i).astype(F32).astype(BF16)
        valid = jnp.dot(mask_t, pick, preferred_element_type=F32)
        masked[core, i] = (n.astype(F32) * valid).astype(BF16)
        return carry

    lax.fori_loop(0, 40, norm_row, 0)
    pl.semaphore_wait(barrier, 2 * CHIPS - 1)

    to_sibling = pltpu.make_async_remote_copy(
        src_ref=masked.at[core],
        dst_ref=masked.at[core],
        send_sem=sibling_send,
        recv_sem=sibling_recv,
        device_id=(r + 1 - 2 * core, c),
        device_id_type=MESH,
    )
    to_sibling.start()

    half = pl.ds(pl.multiple_of(core * 64, 64), 64)
    for n, w in enumerate((proj_w, gate_w)):
        for side in range(2):
            turned = jnp.transpose(w[:, side * 128 : side * 128 + 128].astype(F32))
            finished[0:128, :] = turned
            weights[n * 128 + side * 64 : n * 128 + side * 64 + 64, :] = finished[half, :].astype(BF16)
    to_sibling.wait()

    lane = lax.broadcasted_iota(jnp.int32, (64, 128), 1)

    def project(row, carry):
        who, inner = row // 8, row % 8

        def block(p):
            return masked[who, (p // 5) * 8 + inner, (p % 5) * 16 : (p % 5) * 16 + 16, :]

        tokens = [block(p) for p in range(24)] + [block(24), block(24), jnp.zeros((96, 128), BF16)]
        both = lax.dot_general(weights[...], jnp.concatenate(tokens, axis=0), NT, preferred_element_type=F32)
        value = both[:128] * jax.nn.sigmoid(both[128:])
        for g in range(3):
            wide[pl.ds(g * 16 + row, 64, stride=ROWS), :] = value[:64, g * 128 : g * 128 + 128]
            wide[pl.ds(48 + g * 16 + row, 64, stride=ROWS), :] = value[64:, g * 128 : g * 128 + 128]
        wide[pl.ds(96 + row, 64, stride=ROWS), :] = jnp.where(lane < 16, value[:64, 384:], value[64:, 384:])
        return carry

    lax.fori_loop(0, 16, project, 0)

    def narrow(m, carry):
        packed[m] = wide[pl.ds(pl.multiple_of(m * ROWS, ROWS), ROWS), :].astype(BF16)
        return carry

    lax.fori_loop(0, CHIPS, narrow, 0)

    keep = pltpu.make_async_copy(packed.at[me], arrived.at[me], local)
    keep.start()

    def post(step, carry):
        there = shifted(step)
        pltpu.make_async_remote_copy(
            src_ref=packed.at[chip_index(*there)],
            dst_ref=arrived.at[me],
            send_sem=send,
            recv_sem=recv,
            device_id=device(*there, core),
            device_id_type=MESH,
        ).start()
        return carry

    lax.fori_loop(1, CHIPS, post, 0)

    def gate_row(i, carry):
        gating[i] = jax.nn.sigmoid(jnp.dot(normed[i], out_gate_w[...], preferred_element_type=F32))
        return carry

    lax.fori_loop(0, 40, gate_row, 0)
    for a in range(8):
        at = lax.broadcasted_iota(jnp.int32, (128, 1024), 0)
        to = lax.broadcasted_iota(jnp.int32, (128, 1024), 1)
        swap[a * 128 : a * 128 + 128, :] = (to == (at // 16) * 128 + a * 16 + at % 16).astype(F32).astype(BF16)
    w_t = jnp.transpose(out_w[...].astype(F32))
    shift = lax.dot_general(out_bias[...], w_t, NT, preferred_element_type=F32, precision=lax.Precision.HIGHEST)
    scaled = jnp.transpose(w_t * out_gain[...]).astype(BF16)

    keep.wait()
    whole = pltpu.make_async_remote_copy(
        src_ref=packed.at[pl.ds(0, CHIPS - 1)],
        dst_ref=arrived.at[pl.ds(0, CHIPS - 1)],
        send_sem=send,
        recv_sem=recv,
        device_id=(r + 1 - 2 * core, c),
        device_id_type=MESH,
    )
    whole.wait_recv()

    for g in range(7):
        beside = [
            jnp.concatenate([arrived[m * 8 + k, g * 16 : g * 16 + 16, :] for m in range(8)], axis=0)
            for k in range(8)
        ]
        lanes = 1024 if g < 6 else 256
        moved = jnp.dot(jnp.concatenate(beside, axis=1), swap[:, :lanes], preferred_element_type=F32).astype(BF16)
        for s in range(8 if g < 6 else 2):
            p = (g % 3) * 8 + s if g < 6 else 24
            target = left if (g < 3 or (g == 6 and s == 0)) else right
            target[(p // 5) * 128 : (p // 5) * 128 + 128, (p % 5) * 128 : (p % 5) * 128 + 128] = (
                moved[:, s * 128 : s * 128 + 128]
            )

    for n in range(5):
        rows = pl.ds(n * 128, 128)
        combined[rows, :] = lax.dot_general(left[rows, :], right[...], NT, preferred_element_type=F32).astype(BF16)

    for pair_of in range(2):
        moved = []
        for g in (2 * pair_of, 2 * pair_of + 1):
            blocks = [p for p in range(8 * g, 8 * g + 8) if p < 25]
            beside = [
                combined[(p // 5) * 128 : (p // 5) * 128 + 128, (p % 5) * 128 : (p % 5) * 128 + 128] for p in blocks
            ]
            moved.append(
                jnp.dot(
                    jnp.concatenate(beside, axis=1), swap[: 128 * len(blocks), :], preferred_element_type=F32
                )
            )
        for m in range(8):
            for k in range(8):
                for h in range(2):
                    tile = [v[m * 16 + h * 8 : m * 16 + h * 8 + 8, k * 128 : k * 128 + 128] for v in moved]
                    back[(m * 8 + k) * 2 + h, pair_of * 16 : pair_of * 16 + 16, :] = jnp.concatenate(
                        tile, axis=0
                    ).astype(BF16)

    mine = core * CHIPS + me
    keep_back = pltpu.make_async_copy(back.at[me * 2 + core], returned.at[mine], local)
    keep_back.start()

    def post_back(step, carry):
        there, to_core = shifted(step // 2), (core + step % 2) % 2
        pltpu.make_async_remote_copy(
            src_ref=back.at[chip_index(*there) * 2 + to_core],
            dst_ref=returned.at[mine],
            send_sem=back_send,
            recv_sem=back_recv,
            device_id=device(*there, to_core),
            device_id_type=MESH,
        ).start()
        return carry

    lax.fori_loop(1, 2 * CHIPS, post_back, 0)
    keep_back.wait()
    whole_back = pltpu.make_async_remote_copy(
        src_ref=back.at[pl.ds(0, 2 * CHIPS - 1)],
        dst_ref=returned.at[pl.ds(0, 2 * CHIPS - 1)],
        send_sem=back_send,
        recv_sem=back_recv,
        device_id=(r + 1 - 2 * core, c),
        device_id_type=MESH,
    )
    whole_back.wait_recv()

    def total(ch, carry):
        return carry + returned[ch].astype(F32)

    mean = lax.fori_loop(0, 128, total, jnp.zeros((BACK, 128), F32), unroll=8) * (1 / 128)

    def spread(ch, carry):
        centred = returned[ch].astype(F32) - mean
        return carry + centred * centred

    var = lax.fori_loop(0, 128, spread, jnp.zeros((BACK, 128), F32), unroll=8) * (1 / 128)
    scale = lax.rsqrt(var + 1e-05)

    def normalise(ch, carry):
        finished[pl.ds(pl.multiple_of(ch * BACK, BACK), BACK), :] = (returned[ch].astype(F32) - mean) * scale
        return carry

    lax.fori_loop(0, 128, normalise, 0, unroll=8)

    def finish(inner, carry):
        for g in range(4):
            blocks = [p for p in range(8 * g, 8 * g + 8) if p < 25]
            values = finished[pl.ds(g * 8 + inner, 128, stride=BACK), :]
            tokens = jnp.transpose(values)[: 16 * len(blocks), :].astype(BF16)
            projected = jnp.dot(tokens, scaled, preferred_element_type=F32) + shift
            for s, p in enumerate(blocks):
                at = (p // 5) * 8 + inner
                for h in range(2):
                    cols = pl.ds(h * 40 + (p % 5) * 8, 8)
                    rows = projected[s * 16 + h * 8 : s * 16 + h * 8 + 8, :]
                    out[at, cols, :] = (rows * gating[at, cols, :]).astype(BF16)
        return carry

    lax.fori_loop(0, 8, finish, 0)
    whole.wait_send()
    whole_back.wait_send()


def body(*args):
    pair, mask, norm_gain, norm_bias, proj_w, gate_w, out_gain, out_bias, out_w, out_gate_w = args
    dma = pltpu.SemaphoreType.DMA
    return pl.pallas_call(
        kernel,
        out_shape=jax.ShapeDtypeStruct(pair.shape, BF16),
        in_specs=[pl.BlockSpec(memory_space=pltpu.VMEM)] * 10,
        out_specs=pl.BlockSpec(memory_space=pltpu.VMEM),
        scratch_shapes=[
            pltpu.VMEM((40, 80, 128), BF16),
            pltpu.VMEM((2, 40, 80, 128), BF16),
            pltpu.VMEM((40, 80, 128), F32),
            pltpu.VMEM((256, 128), BF16),
            pltpu.VMEM((CHIPS * ROWS, 128), F32),
            pltpu.VMEM((CHIPS, ROWS, 128), BF16),
            pltpu.VMEM((CHIPS, ROWS, 128), BF16),
            pltpu.VMEM((640, 640), BF16),
            pltpu.VMEM((640, 640), BF16),
            pltpu.VMEM((1024, 1024), BF16),
            pltpu.VMEM((640, 640), BF16),
            pltpu.VMEM((2 * CHIPS, BACK, 128), BF16),
            pltpu.VMEM((2 * CHIPS, BACK, 128), BF16),
            pltpu.VMEM((128 * BACK, 128), F32),
            dma, dma, dma, dma, dma, dma, dma,
        ],
        compiler_params=pltpu.CompilerParams(
            collective_id=0, has_side_effects=True, vmem_limit_bytes=56 * 2**20
        ),
    )(
        pair, mask, norm_gain.reshape(1, 128), norm_bias.reshape(1, 128), proj_w, gate_w,
        out_gain.reshape(1, 128), out_bias.reshape(1, 128), out_w, out_gate_w,
    )


def solution(mesh):
    placed = (P("row", "col", None), P("row", "col"), P(), P(), P(), P(), P(), P(), P(), P())
    return jax.shard_map(body, mesh=mesh, in_specs=placed, out_specs=P("row", "col", None), check_vma=False)
```

```python
import functools

import jax
import jax.numpy as jnp
from jax import lax
from jax.experimental import pallas as pl
from jax.experimental.pallas import tpu as pltpu
from jax.sharding import PartitionSpec as P

MESH = pl.DeviceIdType.MESH
F32, BF16 = jnp.float32, jnp.bfloat16
NT = (((1,), (1,)), ((), ()))
CHIPS = 64
ROWS = 112
BACK = 32


def device(x, y, z, core):
    return (y * 4 + (z // 2) * 2 + core, x * 2 + z % 2)


def chip_index(x, y, z):
    return (y * 2 + z // 2) * 8 + x * 2 + z % 2


def distance(shift):
    return sum(min(d, 4 - d) for d in shift)


SHIFTS = sorted(
    [(n // 16, n // 4 % 4, n % 4) for n in range(1, CHIPS)], key=lambda s: (-distance(s), (s[0] * 7 + s[1] * 11 + s[2] * 13) % 16)
)


def kernel(
    pair, mask, norm_gain, norm_bias, proj_w, gate_w, out_gain, out_bias, out_w, out_gate_w,
    out,
    normed, masked, gating, weights, wide, packed, arrived, left, right, swap, combined, back, returned, finished,
    sibling_send, sibling_recv, send, recv, back_send, back_recv, local, entered_y, entered_z,
):
    r, c = lax.axis_index("row"), lax.axis_index("col")
    x, y, z, core = c // 2, r // 4, ((r // 2) % 2) * 2 + c % 2, r % 2
    me = chip_index(x, y, z)

    def shifted(dx, dy, dz):
        return (x + dx) % 4, (y + dy) % 4, (z + dz) % 4

    barrier = pltpu.get_barrier_semaphore()
    sibling = device(x, y, z, 1 - core)
    along = [[device(*shifted(*(d * (a == n) for a in range(3))), core) for d in (1, 2, 3)] for n in range(3)]
    for there in [sibling] + along[0] + along[1] + along[2]:
        pl.semaphore_signal(barrier, inc=1, device_id=there, device_id_type=MESH)

    def pass_on(sem, line):
        for there in line:
            pl.semaphore_signal(sem, inc=1, device_id=there, device_id_type=MESH)

    swap[0:128, 0:128] = jnp.zeros((128, 128), BF16)
    swap[0:40, 0:80] = mask[...].astype(F32).astype(BF16)
    mask_t = jnp.transpose(swap[0:128, 0:128].astype(F32))[0:80, :].astype(BF16)
    gain, bias = norm_gain[...], norm_bias[...]

    def norm_row(i, carry):
        values = pair[i].astype(F32)
        mean = jnp.mean(values, axis=-1, keepdims=True)
        centred = values - mean
        var = jnp.mean(centred * centred, axis=-1, keepdims=True)
        n = (centred * lax.rsqrt(var + 1e-05) * gain + bias).astype(BF16)
        normed[i] = n
        pick = (lax.broadcasted_iota(jnp.int32, (128, 128), 0) == i).astype(F32).astype(BF16)
        valid = jnp.dot(mask_t, pick, preferred_element_type=F32)
        masked[core, i] = (n.astype(F32) * valid).astype(BF16)
        return carry

    lax.fori_loop(0, 16, norm_row, 0)
    pl.semaphore_wait(barrier, 10)
    pass_on(entered_y, along[1])
    lax.fori_loop(16, 28, norm_row, 0)
    pl.semaphore_wait(entered_y, 3)
    pass_on(entered_z, along[2])
    lax.fori_loop(28, 40, norm_row, 0)
    pl.semaphore_wait(entered_z, 3)

    to_sibling = pltpu.make_async_remote_copy(
        src_ref=masked.at[core],
        dst_ref=masked.at[core],
        send_sem=sibling_send,
        recv_sem=sibling_recv,
        device_id=sibling,
        device_id_type=MESH,
    )
    to_sibling.start()

    half = pl.ds(pl.multiple_of(core * 64, 64), 64)
    for n, w in enumerate((proj_w, gate_w)):
        for side in range(2):
            turned = jnp.transpose(w[:, side * 128 : side * 128 + 128].astype(F32))
            finished[0:128, :] = turned
            weights[n * 128 + side * 64 : n * 128 + side * 64 + 64, :] = finished[half, :].astype(BF16)
    to_sibling.wait()

    lane = lax.broadcasted_iota(jnp.int32, (64, 128), 1)

    def project(row, carry):
        who, inner = row // 8, row % 8

        def block(p):
            return masked[who, (p // 5) * 8 + inner, (p % 5) * 16 : (p % 5) * 16 + 16, :]

        tokens = [block(p) for p in range(24)] + [block(24), block(24), jnp.zeros((96, 128), BF16)]
        both = lax.dot_general(weights[...], jnp.concatenate(tokens, axis=0), NT, preferred_element_type=F32)
        value = both[:128] * jax.nn.sigmoid(both[128:])
        for g in range(3):
            wide[pl.ds(g * 16 + row, 64, stride=ROWS), :] = value[:64, g * 128 : g * 128 + 128]
            wide[pl.ds(48 + g * 16 + row, 64, stride=ROWS), :] = value[64:, g * 128 : g * 128 + 128]
        wide[pl.ds(96 + row, 64, stride=ROWS), :] = jnp.where(lane < 16, value[:64, 384:], value[64:, 384:])
        return carry

    lax.fori_loop(0, 16, project, 0)

    def narrow(m, carry):
        packed[m] = wide[pl.ds(pl.multiple_of(m * ROWS, ROWS), ROWS), :].astype(BF16)
        return carry

    lax.fori_loop(0, CHIPS, narrow, 0)

    keep = pltpu.make_async_copy(packed.at[me], arrived.at[me], local)
    keep.start()

    for shift in SHIFTS:
        there = shifted(*shift)
        pltpu.make_async_remote_copy(
            src_ref=packed.at[chip_index(*there)],
            dst_ref=arrived.at[me],
            send_sem=send,
            recv_sem=recv,
            device_id=device(*there, core),
            device_id_type=MESH,
        ).start()

    def gate_row(i, carry):
        gating[i] = jax.nn.sigmoid(jnp.dot(normed[i], out_gate_w[...], preferred_element_type=F32))
        return carry

    lax.fori_loop(0, 40, gate_row, 0)
    for a in range(8):
        at = lax.broadcasted_iota(jnp.int32, (128, 1024), 0)
        to = lax.broadcasted_iota(jnp.int32, (128, 1024), 1)
        swap[a * 128 : a * 128 + 128, :] = (to == (at // 16) * 128 + a * 16 + at % 16).astype(F32).astype(BF16)
    w_t = jnp.transpose(out_w[...].astype(F32))
    offset = lax.dot_general(out_bias[...], w_t, NT, preferred_element_type=F32, precision=lax.Precision.HIGHEST)
    scaled = jnp.transpose(w_t * out_gain[...]).astype(BF16)

    keep.wait()
    whole = pltpu.make_async_remote_copy(
        src_ref=packed.at[pl.ds(0, CHIPS - 1)],
        dst_ref=arrived.at[pl.ds(0, CHIPS - 1)],
        send_sem=send,
        recv_sem=recv,
        device_id=sibling,
        device_id_type=MESH,
    )
    whole.wait_recv()

    for g in range(7):
        beside = [
            jnp.concatenate([arrived[m * 8 + k, g * 16 : g * 16 + 16, :] for m in range(8)], axis=0)
            for k in range(8)
        ]
        lanes = 1024 if g < 6 else 256
        moved = jnp.dot(jnp.concatenate(beside, axis=1), swap[:, :lanes], preferred_element_type=F32).astype(BF16)
        for s in range(8 if g < 6 else 2):
            p = (g % 3) * 8 + s if g < 6 else 24
            target = left if (g < 3 or (g == 6 and s == 0)) else right
            target[(p // 5) * 128 : (p // 5) * 128 + 128, (p % 5) * 128 : (p % 5) * 128 + 128] = (
                moved[:, s * 128 : s * 128 + 128]
            )

    for n in range(5):
        rows = pl.ds(n * 128, 128)
        combined[rows, :] = lax.dot_general(left[rows, :], right[...], NT, preferred_element_type=F32).astype(BF16)

    for pair_of in range(2):
        moved = []
        for g in (2 * pair_of, 2 * pair_of + 1):
            blocks = [p for p in range(8 * g, 8 * g + 8) if p < 25]
            beside = [
                combined[(p // 5) * 128 : (p // 5) * 128 + 128, (p % 5) * 128 : (p % 5) * 128 + 128] for p in blocks
            ]
            moved.append(
                jnp.dot(
                    jnp.concatenate(beside, axis=1), swap[: 128 * len(blocks), :], preferred_element_type=F32
                )
            )
        for m in range(8):
            for k in range(8):
                for h in range(2):
                    tile = [v[m * 16 + h * 8 : m * 16 + h * 8 + 8, k * 128 : k * 128 + 128] for v in moved]
                    back[(m * 8 + k) * 2 + h, pair_of * 16 : pair_of * 16 + 16, :] = jnp.concatenate(
                        tile, axis=0
                    ).astype(BF16)

    mine = core * CHIPS + me
    keep_back = pltpu.make_async_copy(back.at[me * 2 + core], returned.at[mine], local)
    keep_back.start()

    for shift, other in [(s, o) for s in SHIFTS for o in (0, 1)] + [((0, 0, 0), 1)]:
        there, to_core = shifted(*shift), (core + other) % 2
        pltpu.make_async_remote_copy(
            src_ref=back.at[chip_index(*there) * 2 + to_core],
            dst_ref=returned.at[mine],
            send_sem=back_send,
            recv_sem=back_recv,
            device_id=device(*there, to_core),
            device_id_type=MESH,
        ).start()
    keep_back.wait()
    whole_back = pltpu.make_async_remote_copy(
        src_ref=back.at[pl.ds(0, 2 * CHIPS - 1)],
        dst_ref=returned.at[pl.ds(0, 2 * CHIPS - 1)],
        send_sem=back_send,
        recv_sem=back_recv,
        device_id=sibling,
        device_id_type=MESH,
    )
    whole_back.wait_recv()

    def total(ch, carry):
        return carry + returned[ch].astype(F32)

    mean = lax.fori_loop(0, 128, total, jnp.zeros((BACK, 128), F32), unroll=8) * (1 / 128)

    def spread(ch, carry):
        centred = returned[ch].astype(F32) - mean
        return carry + centred * centred

    var = lax.fori_loop(0, 128, spread, jnp.zeros((BACK, 128), F32), unroll=8) * (1 / 128)
    scale = lax.rsqrt(var + 1e-05)

    def normalise(ch, carry):
        finished[pl.ds(pl.multiple_of(ch * BACK, BACK), BACK), :] = (returned[ch].astype(F32) - mean) * scale
        return carry

    lax.fori_loop(0, 128, normalise, 0, unroll=8)

    def finish(inner, carry):
        for g in range(4):
            blocks = [p for p in range(8 * g, 8 * g + 8) if p < 25]
            values = finished[pl.ds(g * 8 + inner, 128, stride=BACK), :]
            tokens = jnp.transpose(values)[: 16 * len(blocks), :].astype(BF16)
            projected = jnp.dot(tokens, scaled, preferred_element_type=F32) + offset
            for s, p in enumerate(blocks):
                at = (p // 5) * 8 + inner
                for h in range(2):
                    cols = pl.ds(h * 40 + (p % 5) * 8, 8)
                    rows = projected[s * 16 + h * 8 : s * 16 + h * 8 + 8, :]
                    out[at, cols, :] = (rows * gating[at, cols, :]).astype(BF16)
        return carry

    lax.fori_loop(0, 8, finish, 0)
    whole.wait_send()
    whole_back.wait_send()


def body(*args):
    pair, mask, norm_gain, norm_bias, proj_w, gate_w, out_gain, out_bias, out_w, out_gate_w = args
    dma = pltpu.SemaphoreType.DMA
    return pl.pallas_call(
        kernel,
        out_shape=jax.ShapeDtypeStruct(pair.shape, BF16),
        in_specs=[pl.BlockSpec(memory_space=pltpu.VMEM)] * 10,
        out_specs=pl.BlockSpec(memory_space=pltpu.VMEM),
        scratch_shapes=[
            pltpu.VMEM((40, 80, 128), BF16),
            pltpu.VMEM((2, 40, 80, 128), BF16),
            pltpu.VMEM((40, 80, 128), F32),
            pltpu.VMEM((256, 128), BF16),
            pltpu.VMEM((CHIPS * ROWS, 128), F32),
            pltpu.VMEM((CHIPS, ROWS, 128), BF16),
            pltpu.VMEM((CHIPS, ROWS, 128), BF16),
            pltpu.VMEM((640, 640), BF16),
            pltpu.VMEM((640, 640), BF16),
            pltpu.VMEM((1024, 1024), BF16),
            pltpu.VMEM((640, 640), BF16),
            pltpu.VMEM((2 * CHIPS, BACK, 128), BF16),
            pltpu.VMEM((2 * CHIPS, BACK, 128), BF16),
            pltpu.VMEM((128 * BACK, 128), F32),
            dma, dma, dma, dma, dma, dma, dma, pltpu.SemaphoreType.REGULAR, pltpu.SemaphoreType.REGULAR,
        ],
        compiler_params=pltpu.CompilerParams(
            collective_id=0, has_side_effects=True, vmem_limit_bytes=56 * 2**20
        ),
    )(
        pair, mask, norm_gain.reshape(1, 128), norm_bias.reshape(1, 128), proj_w, gate_w,
        out_gain.reshape(1, 128), out_bias.reshape(1, 128), out_w, out_gate_w,
    )


def solution(mesh):
    placed = (P("row", "col", None), P("row", "col"), P(), P(), P(), P(), P(), P(), P(), P())
    return jax.shard_map(body, mesh=mesh, in_specs=placed, out_specs=P("row", "col", None), check_vma=False)
```

```python
import functools

import jax
import jax.numpy as jnp
from jax import lax
from jax.experimental import pallas as pl
from jax.experimental.pallas import tpu as pltpu
from jax.sharding import PartitionSpec as P

MESH = pl.DeviceIdType.MESH
F32, BF16 = jnp.float32, jnp.bfloat16
NT = (((1,), (1,)), ((), ()))
CHIPS = 64
ROWS = 104
BACK = 32


def device(x, y, z, core):
    return (y * 4 + (z // 2) * 2 + core, x * 2 + z % 2)


def chip_index(x, y, z):
    return (y * 2 + z // 2) * 8 + x * 2 + z % 2


def channel_of(x, y, z):
    return x * 16 + y * 4 + z


def distance(shift):
    return sum(min(d, 4 - d) for d in shift)


SHIFTS = sorted(
    [(n // 16, n // 4 % 4, n % 4) for n in range(1, CHIPS)], key=lambda s: (-distance(s), (s[0] * 7 + s[1] * 11 + s[2] * 13) % 16)
)


def kernel(
    pair, mask, norm_gain, norm_bias, proj_w, gate_w, out_gain, out_bias, out_w, out_gate_w,
    out,
    normed, masks, gating, weights, wide, packed, arrived, left, right, swap, combined, back, returned, finished,
    sibling_send, sibling_recv, send, recv, back_send, back_recv, local, entered_y, entered_z,
):
    r, c = lax.axis_index("row"), lax.axis_index("col")
    x, y, z, core = c // 2, r // 4, ((r // 2) % 2) * 2 + c % 2, r % 2
    me, channel = chip_index(x, y, z), channel_of(x, y, z)

    def shifted(dx, dy, dz):
        return (x + dx) % 4, (y + dy) % 4, (z + dz) % 4

    barrier = pltpu.get_barrier_semaphore()
    sibling = device(x, y, z, 1 - core)
    along = [[device(*shifted(*(d * (a == n) for a in range(3))), core) for d in (1, 2, 3)] for n in range(3)]
    for there in [sibling] + along[0] + along[1] + along[2]:
        pl.semaphore_signal(barrier, inc=1, device_id=there, device_id_type=MESH)

    def pass_on(sem, line):
        for there in line:
            pl.semaphore_signal(sem, inc=1, device_id=there, device_id_type=MESH)

    lane = lax.broadcasted_iota(jnp.int32, (8, 128), 1)
    finished[0:40, 0:128] = jnp.zeros((40, 128), F32)
    finished[0:40, 0:80] = mask[...].astype(F32)
    for g in range(3):
        valid = jnp.zeros((8, 128), F32)
        for s in range(8):
            p = 8 * g + s
            turned = pltpu.roll(finished[p // 5 * 8 : p // 5 * 8 + 8, :], (s - p % 5) * 16 % 128, 1)
            valid = jnp.where(lane // 16 == s, turned, valid)
        masks[core, g * 8 : g * 8 + 8, :] = valid
    last = jnp.zeros((8, 128), F32)
    for n in range(8):
        turned = pltpu.roll(jnp.broadcast_to(finished[32 + n : 33 + n, :], (8, 128)), (n - 4) * 16 % 128, 1)
        last = jnp.where(lane // 16 == n, turned, last)
    masks[core, 24:32, :] = last

    gain, bias = norm_gain[...], norm_bias[...]

    def norm_rows(n, carry):
        values = pair[pl.ds(n * 4, 4)].astype(F32)
        mean = jnp.mean(values, axis=-1, keepdims=True)
        centred = values - mean
        var = jnp.mean(centred * centred, axis=-1, keepdims=True)
        normed[core, pl.ds(n * 4, 4)] = (centred * lax.rsqrt(var + 1e-05) * gain + bias).astype(BF16)
        return carry

    def to_sibling(ref, send_sem, recv_sem):
        return pltpu.make_async_remote_copy(
            src_ref=ref, dst_ref=ref, send_sem=send_sem, recv_sem=recv_sem, device_id=sibling, device_id_type=MESH
        )

    exchange = [
        to_sibling(masks.at[core], sibling_send.at[0], sibling_recv.at[0]),
        to_sibling(normed.at[core, pl.ds(0, 20)], sibling_send.at[1], sibling_recv.at[1]),
        to_sibling(normed.at[core, pl.ds(20, 20)], sibling_send.at[2], sibling_recv.at[2]),
    ]
    lax.fori_loop(0, 5, norm_rows, 0)
    pl.semaphore_wait(barrier, 10)
    exchange[0].start()
    exchange[1].start()
    pass_on(entered_y, along[1])
    lax.fori_loop(5, 10, norm_rows, 0)
    exchange[2].start()

    half = pl.ds(pl.multiple_of(core * 64, 64), 64)
    for n, w in enumerate((proj_w, gate_w)):
        for side in range(2):
            finished[0:128, :] = jnp.transpose(w[:, side * 128 : side * 128 + 128].astype(F32))
            mine = finished[half, :].astype(BF16)
            for a in range(4):
                weights[a, (n * 2 + side) * 16 : (n * 2 + side) * 16 + 16, :] = mine[a * 16 : a * 16 + 16, :]

    def project(who, xs):
        both_x = jnp.concatenate([weights[a] for a in xs], axis=0)

        def values_of(tokens, valid):
            got = lax.dot_general(both_x, tokens, NT, preferred_element_type=F32)
            proj = jnp.concatenate([got[0:32], got[64:96]], axis=0)
            gate = jnp.concatenate([got[32:64], got[96:128]], axis=0)
            return proj * (0.5 * jnp.tanh(0.5 * gate) + 0.5) * valid

        def put(values, row, side_rows):
            for n, a in enumerate(xs):
                for side in range(2):
                    wide[pl.ds(a * (16 * ROWS) + side * side_rows + row, 16, stride=ROWS), :] = values[
                        (2 * n + side) * 16 : (2 * n + side) * 16 + 16
                    ]

        def project_row(inner, carry):
            tokens = [
                normed[who, (p // 5) * 8 + inner, (p % 5) * 16 : (p % 5) * 16 + 16, :] for p in range(24)
            ]
            valid = jnp.concatenate([masks[who, pl.ds(g * 8 + inner, 1), :] for g in range(3)], axis=1)
            values = values_of(jnp.concatenate(tokens, axis=0), valid)
            for g in range(3):
                put(values[:, g * 128 : g * 128 + 128], g * 16 + who * 8 + inner, 48)
            return carry

        lax.fori_loop(0, 8, project_row, 0)
        last_tokens = [normed[who, 32 + n, 64:80, :] for n in range(8)]
        put(values_of(jnp.concatenate(last_tokens, axis=0), masks[who, 24:25, :]), 96 + who, 2)

    def narrow(a):
        def one(n, carry):
            m = a * 16 + n
            packed[m] = wide[pl.ds(pl.multiple_of(m * ROWS, 8), ROWS), :].astype(BF16)
            return carry

        lax.fori_loop(0, 16, one, 0, unroll=4)

    def post(dxs):
        for shift in SHIFTS:
            if shift[0] in dxs:
                there = shifted(*shift)
                pltpu.make_async_remote_copy(
                    src_ref=packed.at[channel_of(*there)],
                    dst_ref=arrived.at[me],
                    send_sem=send,
                    recv_sem=recv,
                    device_id=device(*there, core),
                    device_id_type=MESH,
                ).start()

    for row in range(100, ROWS):
        wide[pl.ds(row, CHIPS, stride=ROWS), :] = jnp.zeros((CHIPS, 128), F32)
    for part, dxs in enumerate(((2, 1), (3, 0))):
        xs = [(x + dx) % 4 for dx in dxs]
        project(core, xs)
        if part == 0:
            pl.semaphore_wait(entered_y, 3)
            pass_on(entered_z, along[2])
            for e in exchange:
                e.wait()
        project(1 - core, xs)
        for a in xs:
            narrow(a)
        if part == 0:
            pl.semaphore_wait(entered_z, 3)
        post(dxs)
    keep = pltpu.make_async_copy(packed.at[channel], arrived.at[me], local)
    keep.start()

    def gate_row(i, carry):
        gate = jnp.dot(normed[core, i], out_gate_w[...], preferred_element_type=F32)
        gating[i] = 0.5 * jnp.tanh(0.5 * gate) + 0.5
        return carry

    lax.fori_loop(0, 40, gate_row, 0)
    for a in range(8):
        at = lax.broadcasted_iota(jnp.int32, (128, 1024), 0)
        to = lax.broadcasted_iota(jnp.int32, (128, 1024), 1)
        swap[a * 128 : a * 128 + 128, :] = (to == (at // 16) * 128 + a * 16 + at % 16).astype(F32).astype(BF16)
    w_t = jnp.transpose(out_w[...].astype(F32))
    offset = lax.dot_general(out_bias[...], w_t, NT, preferred_element_type=F32, precision=lax.Precision.HIGHEST)
    scaled = jnp.transpose(w_t * out_gain[...]).astype(BF16)

    keep.wait()
    whole = pltpu.make_async_remote_copy(
        src_ref=packed.at[pl.ds(0, CHIPS - 1)],
        dst_ref=arrived.at[pl.ds(0, CHIPS - 1)],
        send_sem=send,
        recv_sem=recv,
        device_id=sibling,
        device_id_type=MESH,
    )
    whole.wait_recv()

    def beside(rows):
        return jnp.concatenate(
            [jnp.concatenate([arrived[m * 8 + k, rows, :] for m in range(8)], axis=0) for k in range(8)], axis=1
        )

    for g in range(6):
        moved = jnp.dot(beside(slice(g * 16, g * 16 + 16)), swap[...], preferred_element_type=F32).astype(BF16)
        for s in range(8):
            p = (g % 3) * 8 + s
            target = left if g < 3 else right
            target[(p // 5) * 128 : (p // 5) * 128 + 128, (p % 5) * 128 : (p % 5) * 128 + 128] = (
                moved[:, s * 128 : s * 128 + 128]
            )
    moved = jnp.dot(beside(slice(96, 104)), swap[...], preferred_element_type=F32)
    for n in range(8):
        finished[n * 64 : n * 64 + 64, :] = moved[:, n * 128 : n * 128 + 128]
        for side in range(2):
            for h in range(2):
                finished[pl.ds(512 + side * 128 + h * 8 + n, 8, stride=16), :] = finished[
                    pl.ds(n * 64 + side * 2 + h, 8, stride=8), :
                ]
    left[512:640, 512:640] = finished[512:640, :].astype(BF16)
    right[512:640, 512:640] = finished[640:768, :].astype(BF16)

    for n in range(5):
        rows = pl.ds(n * 128, 128)
        combined[rows, :] = lax.dot_general(left[rows, :], right[...], NT, preferred_element_type=F32).astype(BF16)

    for pair_of in range(2):
        moved = []
        for g in (2 * pair_of, 2 * pair_of + 1):
            blocks = [p for p in range(8 * g, 8 * g + 8) if p < 25]
            beside = [
                combined[(p // 5) * 128 : (p // 5) * 128 + 128, (p % 5) * 128 : (p % 5) * 128 + 128] for p in blocks
            ]
            moved.append(
                jnp.dot(
                    jnp.concatenate(beside, axis=1), swap[: 128 * len(blocks), :], preferred_element_type=F32
                )
            )
        for m in range(8):
            for k in range(8):
                for h in range(2):
                    tile = [v[m * 16 + h * 8 : m * 16 + h * 8 + 8, k * 128 : k * 128 + 128] for v in moved]
                    back[(m * 8 + k) * 2 + h, pair_of * 16 : pair_of * 16 + 16, :] = jnp.concatenate(
                        tile, axis=0
                    ).astype(BF16)

    mine = core * CHIPS + channel
    keep_back = pltpu.make_async_copy(back.at[me * 2 + core], returned.at[mine], local)
    keep_back.start()

    for shift, other in [(s, o) for s in SHIFTS for o in (0, 1)] + [((0, 0, 0), 1)]:
        there, to_core = shifted(*shift), (core + other) % 2
        pltpu.make_async_remote_copy(
            src_ref=back.at[chip_index(*there) * 2 + to_core],
            dst_ref=returned.at[mine],
            send_sem=back_send,
            recv_sem=back_recv,
            device_id=device(*there, to_core),
            device_id_type=MESH,
        ).start()
    keep_back.wait()
    whole_back = pltpu.make_async_remote_copy(
        src_ref=back.at[pl.ds(0, 2 * CHIPS - 1)],
        dst_ref=returned.at[pl.ds(0, 2 * CHIPS - 1)],
        send_sem=back_send,
        recv_sem=back_recv,
        device_id=sibling,
        device_id_type=MESH,
    )
    whole_back.wait_recv()

    def total(ch, carry):
        return carry + returned[ch].astype(F32)

    mean = lax.fori_loop(0, 128, total, jnp.zeros((BACK, 128), F32), unroll=8) * (1 / 128)

    def spread(ch, carry):
        centred = returned[ch].astype(F32) - mean
        return carry + centred * centred

    var = lax.fori_loop(0, 128, spread, jnp.zeros((BACK, 128), F32), unroll=8) * (1 / 128)
    scale = lax.rsqrt(var + 1e-05)

    def normalise(ch, carry):
        finished[pl.ds(pl.multiple_of(ch * BACK, BACK), BACK), :] = (returned[ch].astype(F32) - mean) * scale
        return carry

    lax.fori_loop(0, 128, normalise, 0, unroll=8)

    def finish(inner, carry):
        for g in range(4):
            blocks = [p for p in range(8 * g, 8 * g + 8) if p < 25]
            values = finished[pl.ds(g * 8 + inner, 128, stride=BACK), :]
            tokens = jnp.transpose(values)[: 16 * len(blocks), :].astype(BF16)
            projected = jnp.dot(tokens, scaled, preferred_element_type=F32) + offset
            for s, p in enumerate(blocks):
                at = (p // 5) * 8 + inner
                for h in range(2):
                    cols = pl.ds(h * 40 + (p % 5) * 8, 8)
                    rows = projected[s * 16 + h * 8 : s * 16 + h * 8 + 8, :]
                    out[at, cols, :] = (rows * gating[at, cols, :]).astype(BF16)
        return carry

    lax.fori_loop(0, 8, finish, 0)
    whole.wait_send()
    whole_back.wait_send()


def body(*args):
    pair, mask, norm_gain, norm_bias, proj_w, gate_w, out_gain, out_bias, out_w, out_gate_w = args
    dma = pltpu.SemaphoreType.DMA
    return pl.pallas_call(
        kernel,
        out_shape=jax.ShapeDtypeStruct(pair.shape, BF16),
        in_specs=[pl.BlockSpec(memory_space=pltpu.VMEM)] * 10,
        out_specs=pl.BlockSpec(memory_space=pltpu.VMEM),
        scratch_shapes=[
            pltpu.VMEM((2, 40, 80, 128), BF16),
            pltpu.VMEM((2, 32, 128), F32),
            pltpu.VMEM((40, 80, 128), F32),
            pltpu.VMEM((4, 64, 128), BF16),
            pltpu.VMEM((CHIPS * ROWS, 128), F32),
            pltpu.VMEM((CHIPS, ROWS, 128), BF16),
            pltpu.VMEM((CHIPS, ROWS, 128), BF16),
            pltpu.VMEM((640, 640), BF16),
            pltpu.VMEM((640, 640), BF16),
            pltpu.VMEM((1024, 1024), BF16),
            pltpu.VMEM((640, 640), BF16),
            pltpu.VMEM((2 * CHIPS, BACK, 128), BF16),
            pltpu.VMEM((2 * CHIPS, BACK, 128), BF16),
            pltpu.VMEM((128 * BACK, 128), F32),
            pltpu.SemaphoreType.DMA((3,)), pltpu.SemaphoreType.DMA((3,)), dma, dma, dma, dma, dma, pltpu.SemaphoreType.REGULAR, pltpu.SemaphoreType.REGULAR,
        ],
        compiler_params=pltpu.CompilerParams(
            collective_id=0, has_side_effects=True, vmem_limit_bytes=56 * 2**20
        ),
    )(
        pair, mask, norm_gain.reshape(1, 128), norm_bias.reshape(1, 128), proj_w, gate_w,
        out_gain.reshape(1, 128), out_bias.reshape(1, 128), out_w, out_gate_w,
    )


def solution(mesh):
    placed = (P("row", "col", None), P("row", "col"), P(), P(), P(), P(), P(), P(), P(), P())
    return jax.shard_map(body, mesh=mesh, in_specs=placed, out_specs=P("row", "col", None), check_vma=False)
```

```python
import functools

import jax
import jax.numpy as jnp
from jax import lax
from jax.experimental import pallas as pl
from jax.experimental.pallas import tpu as pltpu
from jax.sharding import PartitionSpec as P

MESH = pl.DeviceIdType.MESH
F32, BF16 = jnp.float32, jnp.bfloat16
NT = (((1,), (1,)), ((), ()))
CHIPS = 64
ROWS = 104
BACK = 32


def device(x, y, z, core):
    return (y * 4 + (z // 2) * 2 + core, x * 2 + z % 2)


def chip_index(x, y, z):
    return (y * 2 + z // 2) * 8 + x * 2 + z % 2


def channel_of(x, y, z):
    return x * 16 + y * 4 + z


def distance(shift):
    return sum(min(d, 4 - d) for d in shift)


SHIFTS = sorted(
    [(n // 16, n // 4 % 4, n % 4) for n in range(1, CHIPS)],
    key=lambda s: (-distance(s), -min(s[1], 4 - s[1]), (s[0] * 7 + s[1] * 11 + s[2] * 13) % 16),
)


def kernel(
    pair, mask, norm_gain, norm_bias, proj_w, gate_w, out_gain, out_bias, out_w, out_gate_w,
    out,
    normed, masks, gating, weights, wide, packed, arrived, left, right, swap, combined, back_0, back_1,
    returned_0, returned_1, last_out, last_in, last_gating, finished,
    sibling_send, sibling_recv, send, recv, back_send, back_recv, last_send, last_recv, local, entered_y, entered_z,
):
    r, c = lax.axis_index("row"), lax.axis_index("col")
    x, y, z, core = c // 2, r // 4, ((r // 2) % 2) * 2 + c % 2, r % 2
    me, channel = chip_index(x, y, z), channel_of(x, y, z)

    def shifted(dx, dy, dz):
        return (x + dx) % 4, (y + dy) % 4, (z + dz) % 4

    barrier = pltpu.get_barrier_semaphore()
    sibling = device(x, y, z, 1 - core)
    along = [[device(*shifted(*(d * (a == n) for a in range(3))), core) for d in (1, 2, 3)] for n in range(3)]
    for there in [sibling] + along[0] + along[1] + along[2]:
        pl.semaphore_signal(barrier, inc=1, device_id=there, device_id_type=MESH)

    def pass_on(sem, line):
        for there in line:
            pl.semaphore_signal(sem, inc=1, device_id=there, device_id_type=MESH)

    lane = lax.broadcasted_iota(jnp.int32, (8, 128), 1)
    finished[0:40, 0:128] = jnp.zeros((40, 128), F32)
    finished[0:40, 0:80] = mask[...].astype(F32)
    for g in range(3):
        valid = jnp.zeros((8, 128), F32)
        for s in range(8):
            p = 8 * g + s
            turned = pltpu.roll(finished[p // 5 * 8 : p // 5 * 8 + 8, :], (s - p % 5) * 16 % 128, 1)
            valid = jnp.where(lane // 16 == s, turned, valid)
        masks[core, g * 8 : g * 8 + 8, :] = valid
    last = jnp.zeros((8, 128), F32)
    for n in range(8):
        turned = pltpu.roll(jnp.broadcast_to(finished[32 + n : 33 + n, :], (8, 128)), (n - 4) * 16 % 128, 1)
        last = jnp.where(lane // 16 == n, turned, last)
    masks[core, 24:32, :] = last

    gain, bias = norm_gain[...], norm_bias[...]

    def norm_rows(n, carry):
        values = pair[pl.ds(n * 4, 4)].astype(F32)
        mean = jnp.mean(values, axis=-1, keepdims=True)
        centred = values - mean
        var = jnp.mean(centred * centred, axis=-1, keepdims=True)
        normed[core, pl.ds(n * 4, 4)] = (centred * lax.rsqrt(var + 1e-05) * gain + bias).astype(BF16)
        return carry

    def to_sibling(ref, send_sem, recv_sem):
        return pltpu.make_async_remote_copy(
            src_ref=ref, dst_ref=ref, send_sem=send_sem, recv_sem=recv_sem, device_id=sibling, device_id_type=MESH
        )

    exchange = [
        to_sibling(masks.at[core], sibling_send.at[0], sibling_recv.at[0]),
        to_sibling(normed.at[core, pl.ds(0, 20)], sibling_send.at[1], sibling_recv.at[1]),
        to_sibling(normed.at[core, pl.ds(20, 20)], sibling_send.at[2], sibling_recv.at[2]),
    ]
    lax.fori_loop(0, 5, norm_rows, 0, unroll=5)
    pl.semaphore_wait(barrier, 10)
    exchange[0].start()
    exchange[1].start()
    pass_on(entered_y, along[1])
    lax.fori_loop(5, 10, norm_rows, 0, unroll=5)
    exchange[2].start()

    half = pl.ds(pl.multiple_of(core * 64, 64), 64)
    for n, w in enumerate((proj_w, gate_w)):
        for side in range(2):
            finished[0:128, :] = jnp.transpose(w[:, side * 128 : side * 128 + 128].astype(F32))
            weights[(n * 2 + side) * 64 : (n * 2 + side) * 64 + 64, :] = finished[half, :].astype(BF16)

    def project(who):
        def values_of(tokens, valid):
            got = lax.dot_general(weights[...], tokens, NT, preferred_element_type=F32)
            return got[:128] * (0.5 * jnp.tanh(0.5 * got[128:]) + 0.5) * valid

        def put(values, row, side_rows):
            for side in range(2):
                wide[pl.ds(side * side_rows + row, CHIPS, stride=ROWS), :] = values[side * 64 : side * 64 + 64]

        def project_row(inner, carry):
            tokens = [
                normed[who, (p // 5) * 8 + inner, (p % 5) * 16 : (p % 5) * 16 + 16, :] for p in range(24)
            ]
            valid = jnp.concatenate([masks[who, pl.ds(g * 8 + inner, 1), :] for g in range(3)], axis=1)
            values = values_of(jnp.concatenate(tokens, axis=0), valid)
            for g in range(3):
                put(values[:, g * 128 : g * 128 + 128], g * 16 + who * 8 + inner, 48)
            return carry

        lax.fori_loop(0, 8, project_row, 0, unroll=8)
        last_tokens = [normed[who, 32 + n, 64:80, :] for n in range(8)]
        put(values_of(jnp.concatenate(last_tokens, axis=0), masks[who, 24:25, :]), 96 + who, 2)

    for row in range(100, ROWS):
        wide[pl.ds(row, CHIPS, stride=ROWS), :] = jnp.zeros((CHIPS, 128), F32)
    project(core)
    pl.semaphore_wait(entered_y, 3)
    pass_on(entered_z, along[2])
    for e in exchange:
        e.wait()
    project(1 - core)

    def narrow(m, carry):
        packed[m] = wide[pl.ds(pl.multiple_of(m * ROWS, 8), ROWS), :].astype(BF16)
        return carry

    lax.fori_loop(0, CHIPS, narrow, 0, unroll=4)
    pl.semaphore_wait(entered_z, 3)
    for shift in SHIFTS:
        there = shifted(*shift)
        pltpu.make_async_remote_copy(
            src_ref=packed.at[channel_of(*there)],
            dst_ref=arrived.at[me],
            send_sem=send,
            recv_sem=recv.at[shift[1]],
            device_id=device(*there, core),
            device_id_type=MESH,
        ).start()
    keep = pltpu.make_async_copy(packed.at[channel], arrived.at[me], local)
    keep.start()

    def gate_row(i, carry):
        gate = jnp.dot(normed[core, i], out_gate_w[...], preferred_element_type=F32)
        gating[i] = 0.5 * jnp.tanh(0.5 * gate) + 0.5
        return carry

    lax.fori_loop(0, 40, gate_row, 0)
    for inner in range(8):
        tokens = jnp.concatenate([normed[1, 32 + inner, h * 40 + 32 : h * 40 + 40, :] for h in range(2)], axis=0)
        gate = jnp.dot(tokens, out_gate_w[...], preferred_element_type=F32)
        last_gating[inner] = 0.5 * jnp.tanh(0.5 * gate) + 0.5
    for a in range(8):
        at = lax.broadcasted_iota(jnp.int32, (128, 1024), 0)
        to = lax.broadcasted_iota(jnp.int32, (128, 1024), 1)
        swap[a * 128 : a * 128 + 128, :] = (to == (at // 16) * 128 + a * 16 + at % 16).astype(F32).astype(BF16)
    w_t = jnp.transpose(out_w[...].astype(F32))
    offset = lax.dot_general(out_bias[...], w_t, NT, preferred_element_type=F32, precision=lax.Precision.HIGHEST)
    scaled = jnp.transpose(w_t * out_gain[...]).astype(BF16)

    for dy in (2, 1, 3, 0):
        n_from = 16 if dy else 15
        pltpu.make_async_remote_copy(
            src_ref=packed.at[pl.ds(0, n_from)],
            dst_ref=arrived.at[pl.ds(0, n_from)],
            send_sem=send,
            recv_sem=recv.at[dy],
            device_id=sibling,
            device_id_type=MESH,
        ).wait_recv()
        if dy == 0:
            keep.wait()
        first = (y + 4 - dy) % 4 * 2
        beside = [
            jnp.concatenate([arrived[(first + m) * 8 + k] for m in range(2)], axis=0) for k in range(8)
        ]
        moved = jnp.dot(jnp.concatenate(beside, axis=1), swap[...], preferred_element_type=F32)
        for m in range(2):
            for side, target in enumerate((left, right)):
                for p in range(24):
                    row, col = m * ROWS + side * 48 + p // 8 * 16, p % 8 * 128
                    at = pl.ds(pl.multiple_of(p // 5 * 128 + (first + m) * 16, 16), 16)
                    target[at, p % 5 * 128 : p % 5 * 128 + 128] = moved[row : row + 16, col : col + 128].astype(BF16)
                for n in range(16):
                    row = m * ROWS + 96 + side * 2 + n // 8
                    finished[n : n + 1, :] = moved[row : row + 1, n % 8 * 128 : n % 8 * 128 + 128]
                at = pl.ds(pl.multiple_of(512 + (first + m) * 16, 16), 16)
                target[at, 512:640] = finished[0:16, :].astype(BF16)

    for n in range(5):
        rows = pl.ds(n * 128, 128)
        got = lax.dot_general(left[rows, :], right[...], NT, preferred_element_type=F32)
        combined[rows, :] = got.astype(BF16)
        if n == 4:
            turned = [got[m * 16 + h : m * 16 + h + 8, 512:640] for m in range(8) for h in (8, 0)]
            last_turned = jnp.concatenate(turned, axis=0).astype(BF16)

    moved = []
    for g in range(4):
        blocks = [
            combined[p // 5 * 128 : p // 5 * 128 + 128, p % 5 * 128 : p % 5 * 128 + 128]
            for p in range(8 * g, min(8 * g + 8, 25))
        ] + ([last_turned] if g == 3 else [])
        moved.append(
            jnp.dot(jnp.concatenate(blocks, axis=1), swap[: 128 * len(blocks), :], preferred_element_type=F32)
        )
    for m in range(8):
        for k in range(8):
            for h, (target, groups) in enumerate(((back_0, 4), (back_1, 3))):
                row = m * 16 + h * 8
                tiles = [v[row : row + 8, k * 128 : k * 128 + 128] for v in moved[:groups]]
                target[m * 8 + k] = jnp.concatenate(tiles, axis=0).astype(BF16)

    mine = core * CHIPS + channel
    sides = ((back_0, returned_0, back_send.at[0], back_recv.at[0]), (back_1, returned_1, back_send.at[1], back_recv.at[1]))

    for shift in SHIFTS:
        there = shifted(*shift)
        for to_core, (source, target, send_sem, recv_sem) in enumerate(sides):
            pltpu.make_async_remote_copy(
                src_ref=source.at[chip_index(*there)],
                dst_ref=target.at[mine],
                send_sem=send_sem,
                recv_sem=recv_sem,
                device_id=device(*there, to_core),
                device_id_type=MESH,
            ).start()

    def end(own):
        source, target, send_sem, recv_sem = sides[own]
        other_source, other_target, other_send, other_recv = sides[1 - own]
        groups = 4 - own
        pltpu.make_async_remote_copy(
            src_ref=other_source.at[me],
            dst_ref=other_target.at[mine],
            send_sem=other_send,
            recv_sem=other_recv,
            device_id=sibling,
            device_id_type=MESH,
        ).start()
        keep_back = pltpu.make_async_copy(source.at[me], target.at[mine], local)
        keep_back.start()
        keep_back.wait()

        def whole(refs, sems, n):
            return pltpu.make_async_remote_copy(
                src_ref=refs[0].at[pl.ds(0, n)],
                dst_ref=refs[1].at[pl.ds(0, n)],
                send_sem=sems[0],
                recv_sem=sems[1],
                device_id=sibling,
                device_id_type=MESH,
            )

        whole((target, target), (send_sem, recv_sem), 2 * CHIPS - 1).wait_recv()

        def total(ch, carry):
            return carry + target[ch].astype(F32)

        none = jnp.zeros((groups * 8, 128), F32)
        mean = lax.fori_loop(0, 128, total, none, unroll=16) * (1 / 128)

        def spread(ch, carry):
            centred = target[ch].astype(F32) - mean
            return carry + centred * centred

        var = lax.fori_loop(0, 128, spread, none, unroll=16) * (1 / 128)
        scale = lax.rsqrt(var + 1e-05)

        def normalise(ch, carry):
            finished[pl.ds(pl.multiple_of(ch * BACK, BACK), groups * 8), :] = (target[ch].astype(F32) - mean) * scale
            return carry

        lax.fori_loop(0, 128, normalise, 0, unroll=16)

        def projected(row, n_blocks):
            values = finished[pl.ds(row, 128, stride=BACK), :]
            tokens = jnp.transpose(values)[: 16 * n_blocks, :].astype(BF16)
            return jnp.dot(tokens, scaled, preferred_element_type=F32) + offset

        def put(got, inner, p, s):
            at = p // 5 * 8 + inner
            for h in range(2):
                cols = pl.ds(h * 40 + p % 5 * 8, 8)
                rows = got[s * 16 + h * 8 : s * 16 + h * 8 + 8, :]
                out[at, cols, :] = (rows * gating[at, cols, :]).astype(BF16)

        passed = pltpu.make_async_remote_copy(
            src_ref=last_out,
            dst_ref=last_in,
            send_sem=last_send,
            recv_sem=last_recv,
            device_id=sibling,
            device_id_type=MESH,
        )
        if own == 0:

            def last_row(inner, carry):
                got = projected(24 + inner, 2)
                put(got, inner, 24, 0)
                last_out[inner] = (got[16:32, :] * last_gating[inner]).astype(BF16)
                return carry

            lax.fori_loop(0, 8, last_row, 0, unroll=8)
            passed.start()

        def finish(inner, carry):
            for g in range(3):
                got = projected(g * 8 + inner, 8)
                for s in range(8):
                    put(got, inner, 8 * g + s, s)
            return carry

        lax.fori_loop(0, 8, finish, 0, unroll=4)
        if own == 0:
            passed.wait_send()
        else:
            passed.wait_recv()
            for inner in range(8):
                for h in range(2):
                    out[32 + inner, pl.ds(h * 40 + 32, 8), :] = last_in[inner, h * 8 : h * 8 + 8, :]
        whole((source, source), (send_sem, recv_sem), CHIPS - 1).wait_send()
        whole((other_source, other_source), (other_send, other_recv), CHIPS).wait_send()

    pl.when(core == 0)(functools.partial(end, 0))
    pl.when(core == 1)(functools.partial(end, 1))
    pltpu.make_async_remote_copy(
        src_ref=packed.at[pl.ds(0, CHIPS - 1)],
        dst_ref=arrived.at[pl.ds(0, CHIPS - 1)],
        send_sem=send,
        recv_sem=recv.at[0],
        device_id=sibling,
        device_id_type=MESH,
    ).wait_send()


def body(*args):
    pair, mask, norm_gain, norm_bias, proj_w, gate_w, out_gain, out_bias, out_w, out_gate_w = args
    dma = pltpu.SemaphoreType.DMA
    return pl.pallas_call(
        kernel,
        out_shape=jax.ShapeDtypeStruct(pair.shape, BF16),
        in_specs=[pl.BlockSpec(memory_space=pltpu.VMEM)] * 10,
        out_specs=pl.BlockSpec(memory_space=pltpu.VMEM),
        scratch_shapes=[
            pltpu.VMEM((2, 40, 80, 128), BF16),
            pltpu.VMEM((2, 32, 128), F32),
            pltpu.VMEM((40, 80, 128), F32),
            pltpu.VMEM((256, 128), BF16),
            pltpu.VMEM((CHIPS * ROWS, 128), F32),
            pltpu.VMEM((CHIPS, ROWS, 128), BF16),
            pltpu.VMEM((CHIPS, ROWS, 128), BF16),
            pltpu.VMEM((640, 640), BF16),
            pltpu.VMEM((640, 640), BF16),
            pltpu.VMEM((1024, 1024), BF16),
            pltpu.VMEM((640, 640), BF16),
            pltpu.VMEM((CHIPS, BACK, 128), BF16),
            pltpu.VMEM((CHIPS, BACK - 8, 128), BF16),
            pltpu.VMEM((2 * CHIPS, BACK, 128), BF16),
            pltpu.VMEM((2 * CHIPS, BACK - 8, 128), BF16),
            pltpu.VMEM((8, 16, 128), BF16),
            pltpu.VMEM((8, 16, 128), BF16),
            pltpu.VMEM((8, 16, 128), F32),
            pltpu.VMEM((128 * BACK, 128), F32),
            dma((3,)), dma((3,)), dma, dma((4,)), dma((2,)), dma((2,)), dma, dma, dma, pltpu.SemaphoreType.REGULAR, pltpu.SemaphoreType.REGULAR,
        ],
        compiler_params=pltpu.CompilerParams(
            collective_id=0, has_side_effects=True, vmem_limit_bytes=56 * 2**20
        ),
    )(
        pair, mask, norm_gain.reshape(1, 128), norm_bias.reshape(1, 128), proj_w, gate_w,
        out_gain.reshape(1, 128), out_bias.reshape(1, 128), out_w, out_gate_w,
    )


def solution(mesh):
    placed = (P("row", "col", None), P("row", "col"), P(), P(), P(), P(), P(), P(), P(), P())
    return jax.shard_map(body, mesh=mesh, in_specs=placed, out_specs=P("row", "col", None), check_vma=False)
```

```python
import functools

import jax
import jax.numpy as jnp
from jax import lax
from jax.experimental import pallas as pl
from jax.experimental.pallas import tpu as pltpu
from jax.sharding import PartitionSpec as P

MESH = pl.DeviceIdType.MESH
F32, BF16 = jnp.float32, jnp.bfloat16
NT = (((1,), (1,)), ((), ()))
CHIPS = 64
ROWS = 104
BACK = 32


def device(x, y, z, core):
    return (y * 4 + (z // 2) * 2 + core, x * 2 + z % 2)


def chip_index(x, y, z):
    return (y * 2 + z // 2) * 8 + x * 2 + z % 2


def channel_of(x, y, z):
    return x * 16 + y * 4 + z


def distance(shift):
    return sum(min(d, 4 - d) for d in shift)


SHIFTS = sorted(
    [(n // 16, n // 4 % 4, n % 4) for n in range(1, CHIPS)],
    key=lambda s: (-distance(s), -min(s[1], 4 - s[1]), (s[0] * 7 + s[1] * 11 + s[2] * 13) % 16),
)


def kernel(
    pair, mask, norm_gain, norm_bias, proj_w, gate_w, out_gain, out_bias, out_w, out_gate_w,
    out,
    normed, masks, gating, weights, wide, packed, arrived, left, right, swap, combined, back_0, back_1,
    returned_0, returned_1, last_out, last_in, last_gating, finished,
    sibling_send, sibling_recv, send, recv, back_send, back_recv, last_send, last_recv, local, entered_y, entered_z,
):
    r, c = lax.axis_index("row"), lax.axis_index("col")
    x, y, z, core = c // 2, r // 4, ((r // 2) % 2) * 2 + c % 2, r % 2
    me, channel = chip_index(x, y, z), channel_of(x, y, z)

    def shifted(dx, dy, dz):
        return (x + dx) % 4, (y + dy) % 4, (z + dz) % 4

    barrier = pltpu.get_barrier_semaphore()
    sibling = device(x, y, z, 1 - core)
    along = [[device(*shifted(*(d * (a == n) for a in range(3))), core) for d in (1, 2, 3)] for n in range(3)]
    for there in [sibling] + along[0] + along[1] + along[2]:
        pl.semaphore_signal(barrier, inc=1, device_id=there, device_id_type=MESH)

    def pass_on(sem, line):
        for there in line:
            pl.semaphore_signal(sem, inc=1, device_id=there, device_id_type=MESH)

    lane = lax.broadcasted_iota(jnp.int32, (8, 128), 1)
    finished[0:40, 0:128] = jnp.zeros((40, 128), F32)
    finished[0:40, 0:80] = mask[...].astype(F32)
    for g in range(3):
        valid = jnp.zeros((8, 128), F32)
        for s in range(8):
            p = 8 * g + s
            turned = pltpu.roll(finished[p // 5 * 8 : p // 5 * 8 + 8, :], (s - p % 5) * 16 % 128, 1)
            valid = jnp.where(lane // 16 == s, turned, valid)
        masks[core, g * 8 : g * 8 + 8, :] = valid
    last = jnp.zeros((8, 128), F32)
    for n in range(8):
        turned = pltpu.roll(jnp.broadcast_to(finished[32 + n : 33 + n, :], (8, 128)), (n - 4) * 16 % 128, 1)
        last = jnp.where(lane // 16 == n, turned, last)
    masks[core, 24:32, :] = last

    gain, bias = norm_gain[...], norm_bias[...]

    def norm_rows(n, carry):
        values = pair[pl.ds(n * 4, 4)].astype(F32)
        mean = jnp.mean(values, axis=-1, keepdims=True)
        centred = values - mean
        var = jnp.mean(centred * centred, axis=-1, keepdims=True)
        normed[core, pl.ds(n * 4, 4)] = (centred * lax.rsqrt(var + 1e-05) * gain + bias).astype(BF16)
        return carry

    def to_sibling(ref, send_sem, recv_sem):
        return pltpu.make_async_remote_copy(
            src_ref=ref, dst_ref=ref, send_sem=send_sem, recv_sem=recv_sem, device_id=sibling, device_id_type=MESH
        )

    exchange = [
        to_sibling(masks.at[core], sibling_send.at[0], sibling_recv.at[0]),
        to_sibling(normed.at[core, pl.ds(0, 20)], sibling_send.at[1], sibling_recv.at[1]),
        to_sibling(normed.at[core, pl.ds(20, 20)], sibling_send.at[2], sibling_recv.at[2]),
    ]
    lax.fori_loop(0, 5, norm_rows, 0, unroll=5)
    pl.semaphore_wait(barrier, 10)
    exchange[0].start()
    exchange[1].start()
    pass_on(entered_y, along[0] + along[1] + along[2])
    lax.fori_loop(5, 10, norm_rows, 0, unroll=5)
    exchange[2].start()

    half = pl.ds(pl.multiple_of(core * 64, 64), 64)
    for n, w in enumerate((proj_w, gate_w)):
        for side in range(2):
            finished[0:128, :] = jnp.transpose(w[:, side * 128 : side * 128 + 128].astype(F32))
            weights[(n * 2 + side) * 64 : (n * 2 + side) * 64 + 64, :] = finished[half, :].astype(BF16)

    def project(who):
        def values_of(tokens, valid):
            got = lax.dot_general(weights[...], tokens, NT, preferred_element_type=F32)
            return got[:128] * (0.5 * jnp.tanh(0.5 * got[128:]) + 0.5) * valid

        def put(values, row, side_rows):
            for side in range(2):
                wide[pl.ds(side * side_rows + row, CHIPS, stride=ROWS), :] = values[side * 64 : side * 64 + 64]

        def project_row(inner, carry):
            tokens = [
                normed[who, (p // 5) * 8 + inner, (p % 5) * 16 : (p % 5) * 16 + 16, :] for p in range(24)
            ]
            valid = jnp.concatenate([masks[who, pl.ds(g * 8 + inner, 1), :] for g in range(3)], axis=1)
            values = values_of(jnp.concatenate(tokens, axis=0), valid)
            for g in range(3):
                put(values[:, g * 128 : g * 128 + 128], g * 16 + who * 8 + inner, 48)
            return carry

        lax.fori_loop(0, 8, project_row, 0, unroll=8)
        last_tokens = [normed[who, 32 + n, 64:80, :] for n in range(8)]
        put(values_of(jnp.concatenate(last_tokens, axis=0), masks[who, 24:25, :]), 96 + who, 2)

    for row in range(100, ROWS):
        wide[pl.ds(row, CHIPS, stride=ROWS), :] = jnp.zeros((CHIPS, 128), F32)
    project(core)
    pl.semaphore_wait(entered_y, 9)
    pass_on(entered_z, along[2])
    for e in exchange:
        e.wait()
    project(1 - core)

    def narrow(m, carry):
        packed[m] = wide[pl.ds(pl.multiple_of(m * ROWS, 8), ROWS), :].astype(BF16)
        return carry

    lax.fori_loop(0, CHIPS, narrow, 0, unroll=4)

    def post(shifts):
        for shift in shifts:
            there = shifted(*shift)
            pltpu.make_async_remote_copy(
                src_ref=packed.at[channel_of(*there)],
                dst_ref=arrived.at[me],
                send_sem=send,
                recv_sem=recv.at[shift[1]],
                device_id=device(*there, core),
                device_id_type=MESH,
            ).start()

    early = [s for s in SHIFTS if 0 in s and distance(s) > 2]
    post(early)
    pl.semaphore_wait(entered_z, 3)
    post([s for s in SHIFTS if s not in early])
    keep = pltpu.make_async_copy(packed.at[channel], arrived.at[me], local)
    keep.start()

    def gate_row(i, carry):
        gate = jnp.dot(normed[core, i], out_gate_w[...], preferred_element_type=F32)
        gating[i] = 0.5 * jnp.tanh(0.5 * gate) + 0.5
        return carry

    lax.fori_loop(0, 40, gate_row, 0)
    for inner in range(8):
        tokens = jnp.concatenate([normed[1, 32 + inner, h * 40 + 32 : h * 40 + 40, :] for h in range(2)], axis=0)
        gate = jnp.dot(tokens, out_gate_w[...], preferred_element_type=F32)
        last_gating[inner] = 0.5 * jnp.tanh(0.5 * gate) + 0.5
    for a in range(8):
        at = lax.broadcasted_iota(jnp.int32, (128, 1024), 0)
        to = lax.broadcasted_iota(jnp.int32, (128, 1024), 1)
        swap[a * 128 : a * 128 + 128, :] = (to == (at // 16) * 128 + a * 16 + at % 16).astype(F32).astype(BF16)
    w_t = jnp.transpose(out_w[...].astype(F32))
    offset = lax.dot_general(out_bias[...], w_t, NT, preferred_element_type=F32, precision=lax.Precision.HIGHEST)
    scaled = jnp.transpose(w_t * out_gain[...]).astype(BF16)

    for dy in (2, 1, 3, 0):
        n_from = 16 if dy else 15
        pltpu.make_async_remote_copy(
            src_ref=packed.at[pl.ds(0, n_from)],
            dst_ref=arrived.at[pl.ds(0, n_from)],
            send_sem=send,
            recv_sem=recv.at[dy],
            device_id=sibling,
            device_id_type=MESH,
        ).wait_recv()
        if dy == 0:
            keep.wait()
        first = (y + 4 - dy) % 4 * 2
        beside = [
            jnp.concatenate([arrived[(first + m) * 8 + k] for m in range(2)], axis=0) for k in range(8)
        ]
        moved = jnp.dot(jnp.concatenate(beside, axis=1), swap[...], preferred_element_type=F32)
        for m in range(2):
            for side, target in enumerate((left, right)):
                for p in range(24):
                    row, col = m * ROWS + side * 48 + p // 8 * 16, p % 8 * 128
                    at = pl.ds(pl.multiple_of(p // 5 * 128 + (first + m) * 16, 16), 16)
                    target[at, p % 5 * 128 : p % 5 * 128 + 128] = moved[row : row + 16, col : col + 128].astype(BF16)
                for n in range(16):
                    row = m * ROWS + 96 + side * 2 + n // 8
                    finished[n : n + 1, :] = moved[row : row + 1, n % 8 * 128 : n % 8 * 128 + 128]
                at = pl.ds(pl.multiple_of(512 + (first + m) * 16, 16), 16)
                target[at, 512:640] = finished[0:16, :].astype(BF16)

    for n in range(5):
        rows = pl.ds(n * 128, 128)
        got = lax.dot_general(left[rows, :], right[...], NT, preferred_element_type=F32)
        combined[rows, :] = got.astype(BF16)
        if n == 4:
            turned = [got[m * 16 + h : m * 16 + h + 8, 512:640] for m in range(8) for h in (8, 0)]
            last_turned = jnp.concatenate(turned, axis=0).astype(BF16)

    moved = []
    for g in range(4):
        blocks = [
            combined[p // 5 * 128 : p // 5 * 128 + 128, p % 5 * 128 : p % 5 * 128 + 128]
            for p in range(8 * g, min(8 * g + 8, 25))
        ] + ([last_turned] if g == 3 else [])
        moved.append(
            jnp.dot(jnp.concatenate(blocks, axis=1), swap[: 128 * len(blocks), :], preferred_element_type=F32)
        )
    for m in range(8):
        for k in range(8):
            for h, (target, groups) in enumerate(((back_0, 4), (back_1, 3))):
                row = m * 16 + h * 8
                tiles = [v[row : row + 8, k * 128 : k * 128 + 128] for v in moved[:groups]]
                target[m * 8 + k] = jnp.concatenate(tiles, axis=0).astype(BF16)

    mine = core * CHIPS + channel
    sides = ((back_0, returned_0, back_send.at[0], back_recv.at[0]), (back_1, returned_1, back_send.at[1], back_recv.at[1]))

    for shift in SHIFTS:
        there = shifted(*shift)
        for to_core, (source, target, send_sem, recv_sem) in enumerate(sides):
            pltpu.make_async_remote_copy(
                src_ref=source.at[chip_index(*there)],
                dst_ref=target.at[mine],
                send_sem=send_sem,
                recv_sem=recv_sem,
                device_id=device(*there, to_core),
                device_id_type=MESH,
            ).start()

    def end(own):
        source, target, send_sem, recv_sem = sides[own]
        other_source, other_target, other_send, other_recv = sides[1 - own]
        groups = 4 - own
        pltpu.make_async_remote_copy(
            src_ref=other_source.at[me],
            dst_ref=other_target.at[mine],
            send_sem=other_send,
            recv_sem=other_recv,
            device_id=sibling,
            device_id_type=MESH,
        ).start()
        keep_back = pltpu.make_async_copy(source.at[me], target.at[mine], local)
        keep_back.start()
        keep_back.wait()

        def whole(refs, sems, n):
            return pltpu.make_async_remote_copy(
                src_ref=refs[0].at[pl.ds(0, n)],
                dst_ref=refs[1].at[pl.ds(0, n)],
                send_sem=sems[0],
                recv_sem=sems[1],
                device_id=sibling,
                device_id_type=MESH,
            )

        whole((target, target), (send_sem, recv_sem), 2 * CHIPS - 1).wait_recv()

        def total(ch, carry):
            return carry + target[ch].astype(F32)

        none = jnp.zeros((groups * 8, 128), F32)
        mean = lax.fori_loop(0, 128, total, none, unroll=16) * (1 / 128)

        def spread(ch, carry):
            centred = target[ch].astype(F32) - mean
            return carry + centred * centred

        var = lax.fori_loop(0, 128, spread, none, unroll=16) * (1 / 128)
        scale = lax.rsqrt(var + 1e-05)

        def normalise(ch, carry):
            finished[pl.ds(pl.multiple_of(ch * BACK, BACK), groups * 8), :] = (target[ch].astype(F32) - mean) * scale
            return carry

        lax.fori_loop(0, 128, normalise, 0, unroll=16)

        def projected(row, n_blocks):
            values = finished[pl.ds(row, 128, stride=BACK), :]
            tokens = jnp.transpose(values)[: 16 * n_blocks, :].astype(BF16)
            return jnp.dot(tokens, scaled, preferred_element_type=F32) + offset

        def put(got, inner, p, s):
            at = p // 5 * 8 + inner
            for h in range(2):
                cols = pl.ds(h * 40 + p % 5 * 8, 8)
                rows = got[s * 16 + h * 8 : s * 16 + h * 8 + 8, :]
                out[at, cols, :] = (rows * gating[at, cols, :]).astype(BF16)

        passed = pltpu.make_async_remote_copy(
            src_ref=last_out,
            dst_ref=last_in,
            send_sem=last_send,
            recv_sem=last_recv,
            device_id=sibling,
            device_id_type=MESH,
        )
        if own == 0:

            def last_row(inner, carry):
                got = projected(24 + inner, 2)
                put(got, inner, 24, 0)
                last_out[inner] = (got[16:32, :] * last_gating[inner]).astype(BF16)
                return carry

            lax.fori_loop(0, 8, last_row, 0, unroll=8)
            passed.start()

        def finish(inner, carry):
            for g in range(3):
                got = projected(g * 8 + inner, 8)
                for s in range(8):
                    put(got, inner, 8 * g + s, s)
            return carry

        lax.fori_loop(0, 8, finish, 0, unroll=4)
        if own == 0:
            passed.wait_send()
        else:
            passed.wait_recv()
            for inner in range(8):
                for h in range(2):
                    out[32 + inner, pl.ds(h * 40 + 32, 8), :] = last_in[inner, h * 8 : h * 8 + 8, :]
        whole((source, source), (send_sem, recv_sem), CHIPS - 1).wait_send()
        whole((other_source, other_source), (other_send, other_recv), CHIPS).wait_send()

    pl.when(core == 0)(functools.partial(end, 0))
    pl.when(core == 1)(functools.partial(end, 1))
    pltpu.make_async_remote_copy(
        src_ref=packed.at[pl.ds(0, CHIPS - 1)],
        dst_ref=arrived.at[pl.ds(0, CHIPS - 1)],
        send_sem=send,
        recv_sem=recv.at[0],
        device_id=sibling,
        device_id_type=MESH,
    ).wait_send()


def body(*args):
    pair, mask, norm_gain, norm_bias, proj_w, gate_w, out_gain, out_bias, out_w, out_gate_w = args
    dma = pltpu.SemaphoreType.DMA
    return pl.pallas_call(
        kernel,
        out_shape=pltpu.VMEM(pair.shape, BF16),
        in_specs=[pl.BlockSpec(memory_space=pltpu.VMEM)] * 10,
        out_specs=pl.BlockSpec(memory_space=pltpu.VMEM),
        scratch_shapes=[
            pltpu.VMEM((2, 40, 80, 128), BF16),
            pltpu.VMEM((2, 32, 128), F32),
            pltpu.VMEM((40, 80, 128), F32),
            pltpu.VMEM((256, 128), BF16),
            pltpu.VMEM((CHIPS * ROWS, 128), F32),
            pltpu.VMEM((CHIPS, ROWS, 128), BF16),
            pltpu.VMEM((CHIPS, ROWS, 128), BF16),
            pltpu.VMEM((640, 640), BF16),
            pltpu.VMEM((640, 640), BF16),
            pltpu.VMEM((1024, 1024), BF16),
            pltpu.VMEM((640, 640), BF16),
            pltpu.VMEM((CHIPS, BACK, 128), BF16),
            pltpu.VMEM((CHIPS, BACK - 8, 128), BF16),
            pltpu.VMEM((2 * CHIPS, BACK, 128), BF16),
            pltpu.VMEM((2 * CHIPS, BACK - 8, 128), BF16),
            pltpu.VMEM((8, 16, 128), BF16),
            pltpu.VMEM((8, 16, 128), BF16),
            pltpu.VMEM((8, 16, 128), F32),
            pltpu.VMEM((128 * BACK, 128), F32),
            dma((3,)), dma((3,)), dma, dma((4,)), dma((2,)), dma((2,)), dma, dma, dma, pltpu.SemaphoreType.REGULAR, pltpu.SemaphoreType.REGULAR,
        ],
        compiler_params=pltpu.CompilerParams(
            collective_id=0, has_side_effects=True, vmem_limit_bytes=56 * 2**20
        ),
    )(
        pair, mask, norm_gain.reshape(1, 128), norm_bias.reshape(1, 128), proj_w, gate_w,
        out_gain.reshape(1, 128), out_bias.reshape(1, 128), out_w, out_gate_w,
    )


def solution(mesh):
    placed = (P("row", "col", None), P("row", "col"), P(), P(), P(), P(), P(), P(), P(), P())
    return jax.shard_map(body, mesh=mesh, in_specs=placed, out_specs=P("row", "col", None), check_vma=False)
```

```python
import functools

import jax
import jax.numpy as jnp
from jax import lax
from jax.experimental import pallas as pl
from jax.experimental.pallas import tpu as pltpu
from jax.sharding import PartitionSpec as P

MESH = pl.DeviceIdType.MESH
F32, BF16 = jnp.float32, jnp.bfloat16
NT = (((1,), (1,)), ((), ()))
CHIPS = 64
ROWS = 104
BACK = 32


def device(x, y, z, core):
    return (y * 4 + (z // 2) * 2 + core, x * 2 + z % 2)


def chip_index(x, y, z):
    return (y * 2 + z // 2) * 8 + x * 2 + z % 2


def channel_of(x, y, z):
    return x * 16 + y * 4 + z


def distance(shift):
    return sum(min(d, 4 - d) for d in shift)


SHIFTS = sorted(
    [(n // 16, n // 4 % 4, n % 4) for n in range(1, CHIPS)],
    key=lambda s: (-distance(s), -min(s[1], 4 - s[1]), (s[0] * 7 + s[1] * 11 + s[2] * 13) % 16),
)


def kernel(
    pair_in, mask_in, norm_gain_in, norm_bias_in, proj_w_in, gate_w_in, out_gain_in, out_bias_in, out_w_in, out_gate_w_in,
    out,
    pair, mask, norm_gain, norm_bias, proj_w, gate_w, out_gain, out_bias, out_w, out_gate_w, load,
    normed, masks, gating, weights, wide, packed, arrived, left, right, swap, combined, back_0, back_1,
    returned_0, returned_1, last_out, last_in, last_gating, finished,
    sibling_send, sibling_recv, send, recv, back_send, back_recv, last_send, last_recv, local, entered_y, entered_z,
):
    r, c = lax.axis_index("row"), lax.axis_index("col")
    x, y, z, core = c // 2, r // 4, ((r // 2) % 2) * 2 + c % 2, r % 2
    me, channel = chip_index(x, y, z), channel_of(x, y, z)

    def shifted(dx, dy, dz):
        return (x + dx) % 4, (y + dy) % 4, (z + dz) % 4

    barrier = pltpu.get_barrier_semaphore()
    sibling = device(x, y, z, 1 - core)
    along = [[device(*shifted(*(d * (a == n) for a in range(3))), core) for d in (1, 2, 3)] for n in range(3)]
    for there in [sibling] + along[0] + along[1] + along[2]:
        pl.semaphore_signal(barrier, inc=1, device_id=there, device_id_type=MESH)

    def pass_on(sem, line):
        for there in line:
            pl.semaphore_signal(sem, inc=1, device_id=there, device_id_type=MESH)

    sources = (
        pair_in, mask_in, norm_gain_in, norm_bias_in, proj_w_in, gate_w_in, out_gain_in, out_bias_in, out_w_in, out_gate_w_in
    )
    places = (pair, mask, norm_gain, norm_bias, proj_w, gate_w, out_gain, out_bias, out_w, out_gate_w)
    loads = [pltpu.make_async_copy(a, b, load.at[n]) for n, (a, b) in enumerate(zip(sources, places))]
    for n in (1, 0, 2, 3, 4, 5, 6, 7, 8, 9):
        loads[n].start()
    loads[1].wait()

    lane = lax.broadcasted_iota(jnp.int32, (8, 128), 1)
    finished[0:40, 0:128] = jnp.zeros((40, 128), F32)
    finished[0:40, 0:80] = mask[...].astype(F32)
    for g in range(3):
        valid = jnp.zeros((8, 128), F32)
        for s in range(8):
            p = 8 * g + s
            turned = pltpu.roll(finished[p // 5 * 8 : p // 5 * 8 + 8, :], (s - p % 5) * 16 % 128, 1)
            valid = jnp.where(lane // 16 == s, turned, valid)
        masks[core, g * 8 : g * 8 + 8, :] = valid
    last = jnp.zeros((8, 128), F32)
    for n in range(8):
        turned = pltpu.roll(jnp.broadcast_to(finished[32 + n : 33 + n, :], (8, 128)), (n - 4) * 16 % 128, 1)
        last = jnp.where(lane // 16 == n, turned, last)
    masks[core, 24:32, :] = last

    for n in (0, 2, 3):
        loads[n].wait()
    gain, bias = norm_gain[...], norm_bias[...]

    def norm_rows(n, carry):
        values = pair[pl.ds(n * 4, 4)].astype(F32)
        mean = jnp.mean(values, axis=-1, keepdims=True)
        centred = values - mean
        var = jnp.mean(centred * centred, axis=-1, keepdims=True)
        normed[core, pl.ds(n * 4, 4)] = (centred * lax.rsqrt(var + 1e-05) * gain + bias).astype(BF16)
        return carry

    def to_sibling(ref, send_sem, recv_sem):
        return pltpu.make_async_remote_copy(
            src_ref=ref, dst_ref=ref, send_sem=send_sem, recv_sem=recv_sem, device_id=sibling, device_id_type=MESH
        )

    exchange = [
        to_sibling(masks.at[core], sibling_send.at[0], sibling_recv.at[0]),
        to_sibling(normed.at[core, pl.ds(0, 20)], sibling_send.at[1], sibling_recv.at[1]),
        to_sibling(normed.at[core, pl.ds(20, 20)], sibling_send.at[2], sibling_recv.at[2]),
    ]
    lax.fori_loop(0, 5, norm_rows, 0, unroll=5)
    pl.semaphore_wait(barrier, 10)
    exchange[0].start()
    exchange[1].start()
    pass_on(entered_y, along[0] + along[1] + along[2])
    lax.fori_loop(5, 10, norm_rows, 0, unroll=5)
    exchange[2].start()

    for n in (4, 5, 6, 7, 8, 9):
        loads[n].wait()
    half = pl.ds(pl.multiple_of(core * 64, 64), 64)
    for n, w in enumerate((proj_w, gate_w)):
        for side in range(2):
            finished[0:128, :] = jnp.transpose(w[:, side * 128 : side * 128 + 128].astype(F32))
            weights[(n * 2 + side) * 64 : (n * 2 + side) * 64 + 64, :] = finished[half, :].astype(BF16)

    def project(who):
        def values_of(tokens, valid):
            got = lax.dot_general(weights[...], tokens, NT, preferred_element_type=F32)
            return got[:128] * (0.5 * jnp.tanh(0.5 * got[128:]) + 0.5) * valid

        def put(values, row, side_rows):
            for side in range(2):
                wide[pl.ds(side * side_rows + row, CHIPS, stride=ROWS), :] = values[side * 64 : side * 64 + 64]

        def project_row(inner, carry):
            tokens = [
                normed[who, (p // 5) * 8 + inner, (p % 5) * 16 : (p % 5) * 16 + 16, :] for p in range(24)
            ]
            valid = jnp.concatenate([masks[who, pl.ds(g * 8 + inner, 1), :] for g in range(3)], axis=1)
            values = values_of(jnp.concatenate(tokens, axis=0), valid)
            for g in range(3):
                put(values[:, g * 128 : g * 128 + 128], g * 16 + who * 8 + inner, 48)
            return carry

        lax.fori_loop(0, 8, project_row, 0, unroll=8)
        last_tokens = [normed[who, 32 + n, 64:80, :] for n in range(8)]
        put(values_of(jnp.concatenate(last_tokens, axis=0), masks[who, 24:25, :]), 96 + who, 2)

    for row in range(100, ROWS):
        wide[pl.ds(row, CHIPS, stride=ROWS), :] = jnp.zeros((CHIPS, 128), F32)
    project(core)
    pl.semaphore_wait(entered_y, 9)
    pass_on(entered_z, along[2])
    for e in exchange:
        e.wait()
    project(1 - core)

    def narrow(m, carry):
        packed[m] = wide[pl.ds(pl.multiple_of(m * ROWS, 8), ROWS), :].astype(BF16)
        return carry

    lax.fori_loop(0, CHIPS, narrow, 0, unroll=4)

    def post(shifts):
        for shift in shifts:
            there = shifted(*shift)
            pltpu.make_async_remote_copy(
                src_ref=packed.at[channel_of(*there)],
                dst_ref=arrived.at[me],
                send_sem=send,
                recv_sem=recv.at[shift[1]],
                device_id=device(*there, core),
                device_id_type=MESH,
            ).start()

    early = [s for s in SHIFTS if 0 in s and distance(s) > 2]
    post(early)
    pl.semaphore_wait(entered_z, 3)
    post([s for s in SHIFTS if s not in early])
    keep = pltpu.make_async_copy(packed.at[channel], arrived.at[me], local)
    keep.start()

    def gate_row(i, carry):
        gate = jnp.dot(normed[core, i], out_gate_w[...], preferred_element_type=F32)
        gating[i] = 0.5 * jnp.tanh(0.5 * gate) + 0.5
        return carry

    lax.fori_loop(0, 40, gate_row, 0)
    for inner in range(8):
        tokens = jnp.concatenate([normed[1, 32 + inner, h * 40 + 32 : h * 40 + 40, :] for h in range(2)], axis=0)
        gate = jnp.dot(tokens, out_gate_w[...], preferred_element_type=F32)
        last_gating[inner] = 0.5 * jnp.tanh(0.5 * gate) + 0.5
    for a in range(8):
        at = lax.broadcasted_iota(jnp.int32, (128, 1024), 0)
        to = lax.broadcasted_iota(jnp.int32, (128, 1024), 1)
        swap[a * 128 : a * 128 + 128, :] = (to == (at // 16) * 128 + a * 16 + at % 16).astype(F32).astype(BF16)
    w_t = jnp.transpose(out_w[...].astype(F32))
    offset = lax.dot_general(out_bias[...], w_t, NT, preferred_element_type=F32, precision=lax.Precision.HIGHEST)
    scaled = jnp.transpose(w_t * out_gain[...]).astype(BF16)

    for dy in (2, 1, 3, 0):
        n_from = 16 if dy else 15
        pltpu.make_async_remote_copy(
            src_ref=packed.at[pl.ds(0, n_from)],
            dst_ref=arrived.at[pl.ds(0, n_from)],
            send_sem=send,
            recv_sem=recv.at[dy],
            device_id=sibling,
            device_id_type=MESH,
        ).wait_recv()
        if dy == 0:
            keep.wait()
        first = (y + 4 - dy) % 4 * 2
        beside = [
            jnp.concatenate([arrived[(first + m) * 8 + k] for m in range(2)], axis=0) for k in range(8)
        ]
        moved = jnp.dot(jnp.concatenate(beside, axis=1), swap[...], preferred_element_type=F32)
        for m in range(2):
            for side, target in enumerate((left, right)):
                for p in range(24):
                    row, col = m * ROWS + side * 48 + p // 8 * 16, p % 8 * 128
                    at = pl.ds(pl.multiple_of(p // 5 * 128 + (first + m) * 16, 16), 16)
                    target[at, p % 5 * 128 : p % 5 * 128 + 128] = moved[row : row + 16, col : col + 128].astype(BF16)
                for n in range(16):
                    row = m * ROWS + 96 + side * 2 + n // 8
                    finished[n : n + 1, :] = moved[row : row + 1, n % 8 * 128 : n % 8 * 128 + 128]
                at = pl.ds(pl.multiple_of(512 + (first + m) * 16, 16), 16)
                target[at, 512:640] = finished[0:16, :].astype(BF16)

    got = lax.dot_general(left[...], right[...], NT, preferred_element_type=F32)
    combined[...] = got.astype(BF16)
    turned = [got[512 + m * 16 + h : 512 + m * 16 + h + 8, 512:640] for m in range(8) for h in (8, 0)]
    last_turned = jnp.concatenate(turned, axis=0).astype(BF16)

    def block(p):
        return combined[p // 5 * 128 : p // 5 * 128 + 128, p % 5 * 128 : p % 5 * 128 + 128]

    groups = [jnp.concatenate([block(p) for p in range(8 * g, 8 * g + 8)], axis=1) for g in range(3)]
    moved_3 = jnp.dot(jnp.concatenate(groups, axis=0), swap[...], preferred_element_type=F32)
    last = jnp.concatenate([block(24), last_turned], axis=1)
    moved = [moved_3[g * 128 : g * 128 + 128] for g in range(3)]
    moved.append(jnp.dot(last, swap[0:256, :], preferred_element_type=F32))
    for m in range(8):
        for k in range(8):
            for h, (target, groups) in enumerate(((back_0, 4), (back_1, 3))):
                row = m * 16 + h * 8
                tiles = [v[row : row + 8, k * 128 : k * 128 + 128] for v in moved[:groups]]
                target[m * 8 + k] = jnp.concatenate(tiles, axis=0).astype(BF16)

    mine = core * CHIPS + channel
    sides = ((back_0, returned_0, back_send.at[0], back_recv.at[0]), (back_1, returned_1, back_send.at[1], back_recv.at[1]))

    for shift in SHIFTS:
        there = shifted(*shift)
        for to_core, (source, target, send_sem, recv_sem) in enumerate(sides):
            pltpu.make_async_remote_copy(
                src_ref=source.at[chip_index(*there)],
                dst_ref=target.at[mine],
                send_sem=send_sem,
                recv_sem=recv_sem,
                device_id=device(*there, to_core),
                device_id_type=MESH,
            ).start()

    def end(own):
        source, target, send_sem, recv_sem = sides[own]
        other_source, other_target, other_send, other_recv = sides[1 - own]
        groups = 4 - own
        pltpu.make_async_remote_copy(
            src_ref=other_source.at[me],
            dst_ref=other_target.at[mine],
            send_sem=other_send,
            recv_sem=other_recv,
            device_id=sibling,
            device_id_type=MESH,
        ).start()
        keep_back = pltpu.make_async_copy(source.at[me], target.at[mine], local)
        keep_back.start()
        keep_back.wait()

        def whole(refs, sems, n):
            return pltpu.make_async_remote_copy(
                src_ref=refs[0].at[pl.ds(0, n)],
                dst_ref=refs[1].at[pl.ds(0, n)],
                send_sem=sems[0],
                recv_sem=sems[1],
                device_id=sibling,
                device_id_type=MESH,
            )

        whole((target, target), (send_sem, recv_sem), 2 * CHIPS - 1).wait_recv()

        def total(ch, carry):
            return carry + target[ch].astype(F32)

        none = jnp.zeros((groups * 8, 128), F32)
        mean = lax.fori_loop(0, 128, total, none, unroll=16) * (1 / 128)

        def spread(ch, carry):
            centred = target[ch].astype(F32) - mean
            return carry + centred * centred

        var = lax.fori_loop(0, 128, spread, none, unroll=16) * (1 / 128)
        scale = lax.rsqrt(var + 1e-05)

        def normalise(ch, carry):
            finished[pl.ds(pl.multiple_of(ch * BACK, BACK), groups * 8), :] = (target[ch].astype(F32) - mean) * scale
            return carry

        lax.fori_loop(0, 128, normalise, 0, unroll=16)

        def projected(row, n_blocks):
            values = finished[pl.ds(row, 128, stride=BACK), :]
            tokens = jnp.transpose(values)[: 16 * n_blocks, :].astype(BF16)
            return jnp.dot(tokens, scaled, preferred_element_type=F32) + offset

        def put(got, inner, p, s):
            at = p // 5 * 8 + inner
            for h in range(2):
                cols = pl.ds(h * 40 + p % 5 * 8, 8)
                rows = got[s * 16 + h * 8 : s * 16 + h * 8 + 8, :]
                out[at, cols, :] = (rows * gating[at, cols, :]).astype(BF16)

        passed = pltpu.make_async_remote_copy(
            src_ref=last_out,
            dst_ref=last_in,
            send_sem=last_send,
            recv_sem=last_recv,
            device_id=sibling,
            device_id_type=MESH,
        )
        if own == 0:

            def last_row(inner, carry):
                got = projected(24 + inner, 2)
                put(got, inner, 24, 0)
                last_out[inner] = (got[16:32, :] * last_gating[inner]).astype(BF16)
                return carry

            lax.fori_loop(0, 8, last_row, 0, unroll=8)
            passed.start()

        def finish(inner, carry):
            for g in range(3):
                got = projected(g * 8 + inner, 8)
                for s in range(8):
                    put(got, inner, 8 * g + s, s)
            return carry

        lax.fori_loop(0, 8, finish, 0, unroll=4)
        if own == 0:
            passed.wait_send()
        else:
            passed.wait_recv()
            for inner in range(8):
                for h in range(2):
                    out[32 + inner, pl.ds(h * 40 + 32, 8), :] = last_in[inner, h * 8 : h * 8 + 8, :]
        whole((source, source), (send_sem, recv_sem), CHIPS - 1).wait_send()
        whole((other_source, other_source), (other_send, other_recv), CHIPS).wait_send()

    pl.when(core == 0)(functools.partial(end, 0))
    pl.when(core == 1)(functools.partial(end, 1))
    pltpu.make_async_remote_copy(
        src_ref=packed.at[pl.ds(0, CHIPS - 1)],
        dst_ref=arrived.at[pl.ds(0, CHIPS - 1)],
        send_sem=send,
        recv_sem=recv.at[0],
        device_id=sibling,
        device_id_type=MESH,
    ).wait_send()


def body(*args):
    pair, mask, norm_gain, norm_bias, proj_w, gate_w, out_gain, out_bias, out_w, out_gate_w = args
    operands = (
        pair, mask, norm_gain.reshape(1, 128), norm_bias.reshape(1, 128), proj_w, gate_w,
        out_gain.reshape(1, 128), out_bias.reshape(1, 128), out_w, out_gate_w,
    )
    dma = pltpu.SemaphoreType.DMA
    return pl.pallas_call(
        kernel,
        out_shape=pltpu.VMEM(pair.shape, BF16),
        in_specs=[pl.BlockSpec(memory_space=pl.ANY)] * 10,
        out_specs=pl.BlockSpec(memory_space=pltpu.VMEM),
        scratch_shapes=[pltpu.VMEM(a.shape, a.dtype) for a in operands]
        + [
            dma((10,)),
            pltpu.VMEM((2, 40, 80, 128), BF16),
            pltpu.VMEM((2, 32, 128), F32),
            pltpu.VMEM((40, 80, 128), F32),
            pltpu.VMEM((256, 128), BF16),
            pltpu.VMEM((CHIPS * ROWS, 128), F32),
            pltpu.VMEM((CHIPS, ROWS, 128), BF16),
            pltpu.VMEM((CHIPS, ROWS, 128), BF16),
            pltpu.VMEM((640, 640), BF16),
            pltpu.VMEM((640, 640), BF16),
            pltpu.VMEM((1024, 1024), BF16),
            pltpu.VMEM((640, 640), BF16),
            pltpu.VMEM((CHIPS, BACK, 128), BF16),
            pltpu.VMEM((CHIPS, BACK - 8, 128), BF16),
            pltpu.VMEM((2 * CHIPS, BACK, 128), BF16),
            pltpu.VMEM((2 * CHIPS, BACK - 8, 128), BF16),
            pltpu.VMEM((8, 16, 128), BF16),
            pltpu.VMEM((8, 16, 128), BF16),
            pltpu.VMEM((8, 16, 128), F32),
            pltpu.VMEM((128 * BACK, 128), F32),
            dma((3,)), dma((3,)), dma, dma((4,)), dma((2,)), dma((2,)), dma, dma, dma, pltpu.SemaphoreType.REGULAR, pltpu.SemaphoreType.REGULAR,
        ],
        compiler_params=pltpu.CompilerParams(
            collective_id=0, has_side_effects=True, vmem_limit_bytes=56 * 2**20
        ),
    )(*operands)


def solution(mesh):
    placed = (P("row", "col", None), P("row", "col"), P(), P(), P(), P(), P(), P(), P(), P())
    return jax.shard_map(body, mesh=mesh, in_specs=placed, out_specs=P("row", "col", None), check_vma=False)
```

```python
import functools

import jax
import jax.numpy as jnp
from jax import lax
from jax.experimental import pallas as pl
from jax.experimental.pallas import tpu as pltpu
from jax.sharding import PartitionSpec as P

MESH = pl.DeviceIdType.MESH
F32, BF16 = jnp.float32, jnp.bfloat16
NT = (((1,), (1,)), ((), ()))
CHIPS = 64
ROWS = 104
BACK = 32


def device(x, y, z, core):
    return (y * 4 + (z // 2) * 2 + core, x * 2 + z % 2)


def chip_index(x, y, z):
    return (y * 2 + z // 2) * 8 + x * 2 + z % 2


def channel_of(x, y, z):
    return x * 16 + y * 4 + z


def distance(shift):
    return sum(min(d, 4 - d) for d in shift)


SHIFTS = sorted(
    [(n // 16, n // 4 % 4, n % 4) for n in range(1, CHIPS)],
    key=lambda s: (-distance(s), -min(s[1], 4 - s[1]), (s[0] * 7 + s[1] * 11 + s[2] * 13) % 16),
)


def kernel(
    pair_in, mask_in, norm_gain_in, norm_bias_in, proj_w_in, gate_w_in, out_gain_in, out_bias_in, out_w_in, out_gate_w_in,
    out,
    pair, mask, norm_gain, norm_bias, proj_w, gate_w, out_gain, out_bias, out_w, out_gate_w, load,
    normed, masks, gating, weights, wide, packed, arrived, left, right, swap, combined, back_0, back_1,
    returned_0, returned_1, last_out, last_in, last_gating, finished,
    sibling_send, sibling_recv, send, recv, back_send, back_recv, last_send, last_recv, local, entered_y, entered_z,
):
    r, c = lax.axis_index("row"), lax.axis_index("col")
    x, y, z, core = c // 2, r // 4, ((r // 2) % 2) * 2 + c % 2, r % 2
    me, channel = chip_index(x, y, z), channel_of(x, y, z)

    def shifted(dx, dy, dz):
        return (x + dx) % 4, (y + dy) % 4, (z + dz) % 4

    barrier = pltpu.get_barrier_semaphore()
    sibling = device(x, y, z, 1 - core)
    along = [[device(*shifted(*(d * (a == n) for a in range(3))), core) for d in (1, 2, 3)] for n in range(3)]
    for there in [sibling] + along[0] + along[1] + along[2]:
        pl.semaphore_signal(barrier, inc=1, device_id=there, device_id_type=MESH)

    def pass_on(sem, line):
        for there in line:
            pl.semaphore_signal(sem, inc=1, device_id=there, device_id_type=MESH)

    sources = (
        pair_in, mask_in, norm_gain_in, norm_bias_in, proj_w_in, gate_w_in, out_gain_in, out_bias_in, out_w_in, out_gate_w_in
    )
    places = (pair, mask, norm_gain, norm_bias, proj_w, gate_w, out_gain, out_bias, out_w, out_gate_w)
    loads = [pltpu.make_async_copy(a, b, load.at[n]) for n, (a, b) in enumerate(zip(sources, places))]
    for n in (1, 0, 2, 3, 4, 5, 6, 7, 8, 9):
        loads[n].start()
    loads[1].wait()

    lane = lax.broadcasted_iota(jnp.int32, (8, 128), 1)
    finished[0:40, 0:128] = jnp.zeros((40, 128), F32)
    finished[0:40, 0:80] = mask[...].astype(F32)
    for g in range(3):
        valid = jnp.zeros((8, 128), F32)
        for s in range(8):
            p = 8 * g + s
            turned = pltpu.roll(finished[p // 5 * 8 : p // 5 * 8 + 8, :], (s - p % 5) * 16 % 128, 1)
            valid = jnp.where(lane // 16 == s, turned, valid)
        masks[core, g * 8 : g * 8 + 8, :] = valid
    last = jnp.zeros((8, 128), F32)
    for n in range(8):
        turned = pltpu.roll(jnp.broadcast_to(finished[32 + n : 33 + n, :], (8, 128)), (n - 4) * 16 % 128, 1)
        last = jnp.where(lane // 16 == n, turned, last)
    masks[core, 24:32, :] = last

    for n in (0, 2, 3):
        loads[n].wait()
    gain, bias = norm_gain[...], norm_bias[...]

    def norm_rows(n, carry):
        values = pair[pl.ds(n * 4, 4)].astype(F32)
        mean = jnp.mean(values, axis=-1, keepdims=True)
        centred = values - mean
        var = jnp.mean(centred * centred, axis=-1, keepdims=True)
        normed[core, pl.ds(n * 4, 4)] = (centred * lax.rsqrt(var + 1e-05) * gain + bias).astype(BF16)
        return carry

    def to_sibling(ref, send_sem, recv_sem):
        return pltpu.make_async_remote_copy(
            src_ref=ref, dst_ref=ref, send_sem=send_sem, recv_sem=recv_sem, device_id=sibling, device_id_type=MESH
        )

    exchange = [
        to_sibling(masks.at[core], sibling_send.at[0], sibling_recv.at[0]),
        to_sibling(normed.at[core, pl.ds(0, 20)], sibling_send.at[1], sibling_recv.at[1]),
        to_sibling(normed.at[core, pl.ds(20, 20)], sibling_send.at[2], sibling_recv.at[2]),
    ]
    lax.fori_loop(0, 5, norm_rows, 0, unroll=5)
    pl.semaphore_wait(barrier, 10)
    exchange[0].start()
    exchange[1].start()
    pass_on(entered_y, along[0] + along[1] + along[2])
    lax.fori_loop(5, 10, norm_rows, 0, unroll=5)
    exchange[2].start()

    for n in (4, 5, 6, 7, 8, 9):
        loads[n].wait()
    half = pl.ds(pl.multiple_of(core * 64, 64), 64)
    for n, w in enumerate((proj_w, gate_w)):
        for side in range(2):
            finished[0:128, :] = jnp.transpose(w[:, side * 128 : side * 128 + 128].astype(F32))
            weights[(n * 2 + side) * 64 : (n * 2 + side) * 64 + 64, :] = finished[half, :].astype(BF16)

    def project(who):
        def values_of(tokens, valid):
            got = lax.dot_general(weights[...], tokens, NT, preferred_element_type=F32)
            return got[:128] * (0.5 * jnp.tanh(0.5 * got[128:]) + 0.5) * valid

        def put(values, row, side_rows):
            for side in range(2):
                wide[pl.ds(side * side_rows + row, CHIPS, stride=ROWS), :] = values[side * 64 : side * 64 + 64]

        def project_row(inner, carry):
            tokens = [
                normed[who, (p // 5) * 8 + inner, (p % 5) * 16 : (p % 5) * 16 + 16, :] for p in range(24)
            ]
            valid = jnp.concatenate([masks[who, pl.ds(g * 8 + inner, 1), :] for g in range(3)], axis=1)
            values = values_of(jnp.concatenate(tokens, axis=0), valid)
            for g in range(3):
                put(values[:, g * 128 : g * 128 + 128], g * 16 + who * 8 + inner, 48)
            return carry

        lax.fori_loop(0, 8, project_row, 0, unroll=8)
        last_tokens = [normed[who, 32 + n, 64:80, :] for n in range(8)]
        put(values_of(jnp.concatenate(last_tokens, axis=0), masks[who, 24:25, :]), 96 + who, 2)

    for row in range(100, ROWS):
        wide[pl.ds(row, CHIPS, stride=ROWS), :] = jnp.zeros((CHIPS, 128), F32)
    project(core)
    pl.semaphore_wait(entered_y, 9)
    pass_on(entered_z, along[2])
    for e in exchange:
        e.wait()
    project(1 - core)

    def narrow(m, carry):
        packed[m] = wide[pl.ds(pl.multiple_of(m * ROWS, 8), ROWS), :].astype(BF16)
        return carry

    lax.fori_loop(0, CHIPS, narrow, 0, unroll=4)

    def post(shifts):
        for shift in shifts:
            there = shifted(*shift)
            pltpu.make_async_remote_copy(
                src_ref=packed.at[channel_of(*there)],
                dst_ref=arrived.at[me],
                send_sem=send,
                recv_sem=recv.at[shift[1]],
                device_id=device(*there, core),
                device_id_type=MESH,
            ).start()

    early = [s for s in SHIFTS if 0 in s and distance(s) > 2]
    post(early)
    pl.semaphore_wait(entered_z, 3)
    post([s for s in SHIFTS if s not in early])
    keep = pltpu.make_async_copy(packed.at[channel], arrived.at[me], local)
    keep.start()

    def gate_row(i, carry):
        gate = jnp.dot(normed[core, i], out_gate_w[...], preferred_element_type=F32)
        gating[i] = 0.5 * jnp.tanh(0.5 * gate) + 0.5
        return carry

    lax.fori_loop(0, 40, gate_row, 0)
    for inner in range(8):
        tokens = jnp.concatenate([normed[1, 32 + inner, h * 40 + 32 : h * 40 + 40, :] for h in range(2)], axis=0)
        gate = jnp.dot(tokens, out_gate_w[...], preferred_element_type=F32)
        last_gating[inner] = 0.5 * jnp.tanh(0.5 * gate) + 0.5
    for a in range(8):
        at = lax.broadcasted_iota(jnp.int32, (128, 1024), 0)
        to = lax.broadcasted_iota(jnp.int32, (128, 1024), 1)
        swap[a * 128 : a * 128 + 128, :] = (to == (at // 16) * 128 + a * 16 + at % 16).astype(F32).astype(BF16)
    w_t = jnp.transpose(out_w[...].astype(F32))
    offset = lax.dot_general(out_bias[...], w_t, NT, preferred_element_type=F32, precision=lax.Precision.HIGHEST)
    scaled = jnp.transpose(w_t * out_gain[...]).astype(BF16)

    for dy in (2, 1, 3, 0):
        n_from = 16 if dy else 15
        pltpu.make_async_remote_copy(
            src_ref=packed.at[pl.ds(0, n_from)],
            dst_ref=arrived.at[pl.ds(0, n_from)],
            send_sem=send,
            recv_sem=recv.at[dy],
            device_id=sibling,
            device_id_type=MESH,
        ).wait_recv()
        if dy == 0:
            keep.wait()
        first = (y + 4 - dy) % 4 * 2
        beside = [
            jnp.concatenate([arrived[(first + m) * 8 + k] for m in range(2)], axis=0) for k in range(8)
        ]
        moved = jnp.dot(jnp.concatenate(beside, axis=1), swap[...], preferred_element_type=F32)
        for m in range(2):
            for side, target in enumerate((left, right)):
                for p in range(24):
                    row, col = m * ROWS + side * 48 + p // 8 * 16, p % 8 * 128
                    at = pl.ds(pl.multiple_of(p // 5 * 128 + (first + m) * 16, 16), 16)
                    target[at, p % 5 * 128 : p % 5 * 128 + 128] = moved[row : row + 16, col : col + 128].astype(BF16)
                for n in range(16):
                    row = m * ROWS + 96 + side * 2 + n // 8
                    finished[n : n + 1, :] = moved[row : row + 1, n % 8 * 128 : n % 8 * 128 + 128]
                at = pl.ds(pl.multiple_of(512 + (first + m) * 16, 16), 16)
                target[at, 512:640] = finished[0:16, :].astype(BF16)

    got = lax.dot_general(left[...], right[...], NT, preferred_element_type=F32)
    combined[...] = got.astype(BF16)
    turned = [got[512 + m * 16 + h : 512 + m * 16 + h + 8, 512:640] for m in range(8) for h in (8, 0)]
    last_turned = jnp.concatenate(turned, axis=0).astype(BF16)

    def block(p):
        return combined[p // 5 * 128 : p // 5 * 128 + 128, p % 5 * 128 : p % 5 * 128 + 128]

    groups = [jnp.concatenate([block(p) for p in range(8 * g, 8 * g + 8)], axis=1) for g in range(3)]
    moved_3 = jnp.dot(jnp.concatenate(groups, axis=0), swap[...], preferred_element_type=F32)
    last = jnp.concatenate([block(24), last_turned], axis=1)
    moved = [moved_3[g * 128 : g * 128 + 128] for g in range(3)]
    moved.append(jnp.dot(last, swap[0:256, :], preferred_element_type=F32))
    for m in range(8):
        for k in range(8):
            for h, (target, groups) in enumerate(((back_0, 4), (back_1, 3))):
                row = m * 16 + h * 8
                tiles = [v[row : row + 8, k * 128 : k * 128 + 128] for v in moved[:groups]]
                target[m * 8 + k] = jnp.concatenate(tiles, axis=0).astype(BF16)

    mine = core * CHIPS + channel
    sides = ((back_0, returned_0, back_send.at[0], back_recv.at[0]), (back_1, returned_1, back_send.at[1], back_recv.at[1]))

    for shift in SHIFTS:
        there = shifted(*shift)
        for to_core, (source, target, send_sem, recv_sem) in enumerate(sides):
            pltpu.make_async_remote_copy(
                src_ref=source.at[chip_index(*there)],
                dst_ref=target.at[mine],
                send_sem=send_sem,
                recv_sem=recv_sem,
                device_id=device(*there, to_core),
                device_id_type=MESH,
            ).start()

    def end(own):
        source, target, send_sem, recv_sem = sides[own]
        other_source, other_target, other_send, other_recv = sides[1 - own]
        groups = 4 - own
        pltpu.make_async_remote_copy(
            src_ref=other_source.at[me],
            dst_ref=other_target.at[mine],
            send_sem=other_send,
            recv_sem=other_recv,
            device_id=sibling,
            device_id_type=MESH,
        ).start()
        keep_back = pltpu.make_async_copy(source.at[me], target.at[mine], local)
        keep_back.start()
        keep_back.wait()

        def whole(refs, sems, n):
            return pltpu.make_async_remote_copy(
                src_ref=refs[0].at[pl.ds(0, n)],
                dst_ref=refs[1].at[pl.ds(0, n)],
                send_sem=sems[0],
                recv_sem=sems[1],
                device_id=sibling,
                device_id_type=MESH,
            )

        whole((target, target), (send_sem, recv_sem), 2 * CHIPS - 1).wait_recv()

        def total(ch, carry):
            return carry + target[ch].astype(F32)

        none = jnp.zeros((groups * 8, 128), F32)
        middle = lax.fori_loop(0, 32, total, none, unroll=16) * (1 / 32)

        def spread(ch, sums):
            centred = target[ch].astype(F32) - middle
            return sums[0] + centred, sums[1] + centred * centred

        moved_by, var = lax.fori_loop(0, 128, spread, (none, none), unroll=16)
        moved_by = moved_by * (1 / 128)
        mean = middle + moved_by
        var = jnp.maximum(var * (1 / 128) - moved_by * moved_by, 0.0)
        scale = lax.rsqrt(var + 1e-05)

        def normalise(ch, carry):
            finished[pl.ds(pl.multiple_of(ch * BACK, BACK), groups * 8), :] = (target[ch].astype(F32) - mean) * scale
            return carry

        lax.fori_loop(0, 128, normalise, 0, unroll=16)

        def projected(row, n_blocks):
            values = finished[pl.ds(row, 128, stride=BACK), :]
            tokens = jnp.transpose(values)[: 16 * n_blocks, :].astype(BF16)
            return jnp.dot(tokens, scaled, preferred_element_type=F32) + offset

        def put(got, inner, p, s):
            at = p // 5 * 8 + inner
            for h in range(2):
                cols = pl.ds(h * 40 + p % 5 * 8, 8)
                rows = got[s * 16 + h * 8 : s * 16 + h * 8 + 8, :]
                out[at, cols, :] = (rows * gating[at, cols, :]).astype(BF16)

        passed = pltpu.make_async_remote_copy(
            src_ref=last_out,
            dst_ref=last_in,
            send_sem=last_send,
            recv_sem=last_recv,
            device_id=sibling,
            device_id_type=MESH,
        )
        if own == 0:

            def last_row(inner, carry):
                got = projected(24 + inner, 2)
                put(got, inner, 24, 0)
                last_out[inner] = (got[16:32, :] * last_gating[inner]).astype(BF16)
                return carry

            lax.fori_loop(0, 8, last_row, 0, unroll=8)
            passed.start()

        def finish(inner, carry):
            for g in range(3):
                got = projected(g * 8 + inner, 8)
                for s in range(8):
                    put(got, inner, 8 * g + s, s)
            return carry

        lax.fori_loop(0, 8, finish, 0, unroll=4)
        if own == 0:
            passed.wait_send()
        else:
            passed.wait_recv()
            for inner in range(8):
                for h in range(2):
                    out[32 + inner, pl.ds(h * 40 + 32, 8), :] = last_in[inner, h * 8 : h * 8 + 8, :]
        whole((source, source), (send_sem, recv_sem), CHIPS - 1).wait_send()
        whole((other_source, other_source), (other_send, other_recv), CHIPS).wait_send()

    pl.when(core == 0)(functools.partial(end, 0))
    pl.when(core == 1)(functools.partial(end, 1))
    pltpu.make_async_remote_copy(
        src_ref=packed.at[pl.ds(0, CHIPS - 1)],
        dst_ref=arrived.at[pl.ds(0, CHIPS - 1)],
        send_sem=send,
        recv_sem=recv.at[0],
        device_id=sibling,
        device_id_type=MESH,
    ).wait_send()


def body(*args):
    pair, mask, norm_gain, norm_bias, proj_w, gate_w, out_gain, out_bias, out_w, out_gate_w = args
    operands = (
        pair, mask, norm_gain.reshape(1, 128), norm_bias.reshape(1, 128), proj_w, gate_w,
        out_gain.reshape(1, 128), out_bias.reshape(1, 128), out_w, out_gate_w,
    )
    dma = pltpu.SemaphoreType.DMA
    return pl.pallas_call(
        kernel,
        out_shape=pltpu.VMEM(pair.shape, BF16),
        in_specs=[pl.BlockSpec(memory_space=pl.ANY)] * 10,
        out_specs=pl.BlockSpec(memory_space=pltpu.VMEM),
        scratch_shapes=[pltpu.VMEM(a.shape, a.dtype) for a in operands]
        + [
            dma((10,)),
            pltpu.VMEM((2, 40, 80, 128), BF16),
            pltpu.VMEM((2, 32, 128), F32),
            pltpu.VMEM((40, 80, 128), F32),
            pltpu.VMEM((256, 128), BF16),
            pltpu.VMEM((CHIPS * ROWS + ROWS, 128), F32),
            pltpu.VMEM((CHIPS, ROWS, 128), BF16),
            pltpu.VMEM((CHIPS, ROWS, 128), BF16),
            pltpu.VMEM((640, 640), BF16),
            pltpu.VMEM((640, 640), BF16),
            pltpu.VMEM((1024, 1024), BF16),
            pltpu.VMEM((640, 640), BF16),
            pltpu.VMEM((CHIPS, BACK, 128), BF16),
            pltpu.VMEM((CHIPS, BACK - 8, 128), BF16),
            pltpu.VMEM((2 * CHIPS, BACK, 128), BF16),
            pltpu.VMEM((2 * CHIPS, BACK - 8, 128), BF16),
            pltpu.VMEM((8, 16, 128), BF16),
            pltpu.VMEM((8, 16, 128), BF16),
            pltpu.VMEM((8, 16, 128), F32),
            pltpu.VMEM((128 * BACK + BACK, 128), F32),
            dma((3,)), dma((3,)), dma, dma((4,)), dma((2,)), dma((2,)), dma, dma, dma, pltpu.SemaphoreType.REGULAR, pltpu.SemaphoreType.REGULAR,
        ],
        compiler_params=pltpu.CompilerParams(
            collective_id=0, has_side_effects=True, vmem_limit_bytes=56 * 2**20
        ),
    )(*operands)


def solution(mesh):
    placed = (P("row", "col", None), P("row", "col"), P(), P(), P(), P(), P(), P(), P(), P())
    return jax.shard_map(body, mesh=mesh, in_specs=placed, out_specs=P("row", "col", None), check_vma=False)
```

```python
import functools

import jax
import jax.numpy as jnp
from jax import lax
from jax.experimental import pallas as pl
from jax.experimental.pallas import tpu as pltpu
from jax.sharding import PartitionSpec as P

MESH = pl.DeviceIdType.MESH
F32, BF16 = jnp.float32, jnp.bfloat16
NT = (((1,), (1,)), ((), ()))
CHIPS = 64
ROWS = 104
BACK = 32


def device(x, y, z, core):
    return (y * 4 + (z // 2) * 2 + core, x * 2 + z % 2)


def chip_index(x, y, z):
    return (y * 2 + z // 2) * 8 + x * 2 + z % 2


def channel_of(x, y, z):
    return x * 16 + y * 4 + z


def distance(shift):
    return sum(min(d, 4 - d) for d in shift)


SHIFTS = sorted(
    [(n // 16, n // 4 % 4, n % 4) for n in range(1, CHIPS)],
    key=lambda s: (-max(distance(s), 2), -min(s[1], 4 - s[1]), -distance(s), (s[0] * 7 + s[1] * 11 + s[2] * 13) % 16),
)


def kernel(
    pair_in, mask_in, norm_gain_in, norm_bias_in, proj_w_in, gate_w_in, out_gain_in, out_bias_in, out_w_in, out_gate_w_in,
    out,
    pair, mask, norm_gain, norm_bias, proj_w, gate_w, out_gain, out_bias, out_w, out_gate_w, load,
    normed, masks, gating, weights, wide, packed, arrived, left, right, swap, combined, back_0, back_1,
    returned_0, returned_1, last_out, last_in, last_gating, finished,
    sibling_send, sibling_recv, send, recv, back_send, back_recv, last_send, last_recv, local, entered_y, entered_z,
):
    r, c = lax.axis_index("row"), lax.axis_index("col")
    x, y, z, core = c // 2, r // 4, ((r // 2) % 2) * 2 + c % 2, r % 2
    me, channel = chip_index(x, y, z), channel_of(x, y, z)

    def shifted(dx, dy, dz):
        return (x + dx) % 4, (y + dy) % 4, (z + dz) % 4

    barrier = pltpu.get_barrier_semaphore()
    sibling = device(x, y, z, 1 - core)
    along = [[device(*shifted(*(d * (a == n) for a in range(3))), core) for d in (1, 2, 3)] for n in range(3)]
    for there in [sibling] + along[0] + along[1] + along[2]:
        pl.semaphore_signal(barrier, inc=1, device_id=there, device_id_type=MESH)

    def pass_on(sem, line):
        for there in line:
            pl.semaphore_signal(sem, inc=1, device_id=there, device_id_type=MESH)

    sources = (
        pair_in, mask_in, norm_gain_in, norm_bias_in, proj_w_in, gate_w_in, out_gain_in, out_bias_in, out_w_in, out_gate_w_in
    )
    places = (pair, mask, norm_gain, norm_bias, proj_w, gate_w, out_gain, out_bias, out_w, out_gate_w)
    loads = [pltpu.make_async_copy(a, b, load.at[n]) for n, (a, b) in enumerate(zip(sources, places))]
    for n in (1, 0, 2, 3, 4, 5, 6, 7, 8, 9):
        loads[n].start()
    loads[1].wait()

    lane = lax.broadcasted_iota(jnp.int32, (8, 128), 1)
    finished[0:40, 0:128] = jnp.zeros((40, 128), F32)
    finished[0:40, 0:80] = mask[...].astype(F32)
    for g in range(3):
        valid = jnp.zeros((8, 128), F32)
        for s in range(8):
            p = 8 * g + s
            turned = pltpu.roll(finished[p // 5 * 8 : p // 5 * 8 + 8, :], (s - p % 5) * 16 % 128, 1)
            valid = jnp.where(lane // 16 == s, turned, valid)
        masks[core, g * 8 : g * 8 + 8, :] = valid
    last = jnp.zeros((8, 128), F32)
    for n in range(8):
        turned = pltpu.roll(jnp.broadcast_to(finished[32 + n : 33 + n, :], (8, 128)), (n - 4) * 16 % 128, 1)
        last = jnp.where(lane // 16 == n, turned, last)
    masks[core, 24:32, :] = last

    for n in (0, 2, 3):
        loads[n].wait()
    gain, bias = norm_gain[...], norm_bias[...]

    def norm_rows(n, carry):
        values = pair[pl.ds(n * 4, 4)].astype(F32)
        mean = jnp.mean(values, axis=-1, keepdims=True)
        centred = values - mean
        var = jnp.mean(centred * centred, axis=-1, keepdims=True)
        normed[core, pl.ds(n * 4, 4)] = (centred * lax.rsqrt(var + 1e-05) * gain + bias).astype(BF16)
        return carry

    def to_sibling(ref, send_sem, recv_sem):
        return pltpu.make_async_remote_copy(
            src_ref=ref, dst_ref=ref, send_sem=send_sem, recv_sem=recv_sem, device_id=sibling, device_id_type=MESH
        )

    exchange = [
        to_sibling(masks.at[core], sibling_send.at[0], sibling_recv.at[0]),
        to_sibling(normed.at[core, pl.ds(0, 20)], sibling_send.at[1], sibling_recv.at[1]),
        to_sibling(normed.at[core, pl.ds(20, 20)], sibling_send.at[2], sibling_recv.at[2]),
    ]
    lax.fori_loop(0, 5, norm_rows, 0, unroll=5)
    pl.semaphore_wait(barrier, 10)
    exchange[0].start()
    exchange[1].start()
    pass_on(entered_y, along[0] + along[1] + along[2])
    lax.fori_loop(5, 10, norm_rows, 0, unroll=5)
    exchange[2].start()

    for n in (4, 5, 6, 7, 8, 9):
        loads[n].wait()
    half = pl.ds(pl.multiple_of(core * 64, 64), 64)
    for n, w in enumerate((proj_w, gate_w)):
        for side in range(2):
            finished[0:128, :] = jnp.transpose(w[:, side * 128 : side * 128 + 128].astype(F32))
            weights[(n * 2 + side) * 64 : (n * 2 + side) * 64 + 64, :] = finished[half, :].astype(BF16)

    def project(who):
        def values_of(tokens, valid):
            got = lax.dot_general(weights[...], tokens, NT, preferred_element_type=F32)
            return got[:128] * (0.5 * jnp.tanh(0.5 * got[128:]) + 0.5) * valid

        def put(values, row, side_rows):
            for side in range(2):
                wide[pl.ds(side * side_rows + row, CHIPS, stride=ROWS), :] = values[side * 64 : side * 64 + 64]

        def project_row(inner, carry):
            tokens = [
                normed[who, (p // 5) * 8 + inner, (p % 5) * 16 : (p % 5) * 16 + 16, :] for p in range(24)
            ]
            valid = jnp.concatenate([masks[who, pl.ds(g * 8 + inner, 1), :] for g in range(3)], axis=1)
            values = values_of(jnp.concatenate(tokens, axis=0), valid)
            for g in range(3):
                put(values[:, g * 128 : g * 128 + 128], g * 16 + who * 8 + inner, 48)
            return carry

        lax.fori_loop(0, 8, project_row, 0, unroll=8)
        last_tokens = [normed[who, 32 + n, 64:80, :] for n in range(8)]
        put(values_of(jnp.concatenate(last_tokens, axis=0), masks[who, 24:25, :]), 96 + who, 2)

    for row in range(100, ROWS):
        wide[pl.ds(row, CHIPS, stride=ROWS), :] = jnp.zeros((CHIPS, 128), F32)
    project(core)
    pl.semaphore_wait(entered_y, 9)
    pass_on(entered_z, along[2])
    for e in exchange:
        e.wait()
    project(1 - core)

    def narrow(m, carry):
        packed[m] = wide[pl.ds(pl.multiple_of(m * ROWS, 8), ROWS), :].astype(BF16)
        return carry

    lax.fori_loop(0, CHIPS, narrow, 0, unroll=4)

    def post(shifts):
        for shift in shifts:
            there = shifted(*shift)
            pltpu.make_async_remote_copy(
                src_ref=packed.at[channel_of(*there)],
                dst_ref=arrived.at[me],
                send_sem=send,
                recv_sem=recv.at[shift[1]],
                device_id=device(*there, core),
                device_id_type=MESH,
            ).start()

    early = [s for s in SHIFTS if 0 in s and distance(s) > 2]
    post(early)
    pl.semaphore_wait(entered_z, 3)
    post([s for s in SHIFTS if s not in early])
    keep = pltpu.make_async_copy(packed.at[channel], arrived.at[me], local)
    keep.start()

    def gate_row(i, carry):
        gate = jnp.dot(normed[core, i], out_gate_w[...], preferred_element_type=F32)
        gating[i] = 0.5 * jnp.tanh(0.5 * gate) + 0.5
        return carry

    lax.fori_loop(0, 40, gate_row, 0)
    for inner in range(8):
        tokens = jnp.concatenate([normed[1, 32 + inner, h * 40 + 32 : h * 40 + 40, :] for h in range(2)], axis=0)
        gate = jnp.dot(tokens, out_gate_w[...], preferred_element_type=F32)
        last_gating[inner] = 0.5 * jnp.tanh(0.5 * gate) + 0.5
    for a in range(8):
        at = lax.broadcasted_iota(jnp.int32, (128, 1024), 0)
        to = lax.broadcasted_iota(jnp.int32, (128, 1024), 1)
        swap[a * 128 : a * 128 + 128, :] = (to == (at // 16) * 128 + a * 16 + at % 16).astype(F32).astype(BF16)
    w_t = jnp.transpose(out_w[...].astype(F32))
    offset = lax.dot_general(out_bias[...], w_t, NT, preferred_element_type=F32, precision=lax.Precision.HIGHEST)
    scaled = jnp.transpose(w_t * out_gain[...]).astype(BF16)

    for dy in (2, 1, 3, 0):
        n_from = 16 if dy else 15
        pltpu.make_async_remote_copy(
            src_ref=packed.at[pl.ds(0, n_from)],
            dst_ref=arrived.at[pl.ds(0, n_from)],
            send_sem=send,
            recv_sem=recv.at[dy],
            device_id=sibling,
            device_id_type=MESH,
        ).wait_recv()
        if dy == 0:
            keep.wait()
        first = (y + 4 - dy) % 4 * 2
        beside = [
            jnp.concatenate([arrived[(first + m) * 8 + k] for m in range(2)], axis=0) for k in range(8)
        ]
        moved = jnp.dot(jnp.concatenate(beside, axis=1), swap[...], preferred_element_type=F32)
        for m in range(2):
            for side, target in enumerate((left, right)):
                for p in range(24):
                    row, col = m * ROWS + side * 48 + p // 8 * 16, p % 8 * 128
                    at = pl.ds(pl.multiple_of(p // 5 * 128 + (first + m) * 16, 16), 16)
                    target[at, p % 5 * 128 : p % 5 * 128 + 128] = moved[row : row + 16, col : col + 128].astype(BF16)
                for n in range(16):
                    row = m * ROWS + 96 + side * 2 + n // 8
                    finished[n : n + 1, :] = moved[row : row + 1, n % 8 * 128 : n % 8 * 128 + 128]
                at = pl.ds(pl.multiple_of(512 + (first + m) * 16, 16), 16)
                target[at, 512:640] = finished[0:16, :].astype(BF16)

    got = lax.dot_general(left[...], right[...], NT, preferred_element_type=F32)
    combined[...] = got.astype(BF16)
    turned = [got[512 + m * 16 + h : 512 + m * 16 + h + 8, 512:640] for m in range(8) for h in (8, 0)]
    last_turned = jnp.concatenate(turned, axis=0).astype(BF16)

    def block(p):
        return combined[p // 5 * 128 : p // 5 * 128 + 128, p % 5 * 128 : p % 5 * 128 + 128]

    groups = [jnp.concatenate([block(p) for p in range(8 * g, 8 * g + 8)], axis=1) for g in range(3)]
    moved_3 = jnp.dot(jnp.concatenate(groups, axis=0), swap[...], preferred_element_type=F32)
    last = jnp.concatenate([block(24), last_turned], axis=1)
    moved = [moved_3[g * 128 : g * 128 + 128] for g in range(3)]
    moved.append(jnp.dot(last, swap[0:256, :], preferred_element_type=F32))
    for m in range(8):
        for k in range(8):
            for h, (target, groups) in enumerate(((back_0, 4), (back_1, 3))):
                row = m * 16 + h * 8
                tiles = [v[row : row + 8, k * 128 : k * 128 + 128] for v in moved[:groups]]
                target[m * 8 + k] = jnp.concatenate(tiles, axis=0).astype(BF16)

    mine = core * CHIPS + channel
    sides = ((back_0, returned_0, back_send.at[0], back_recv.at[0]), (back_1, returned_1, back_send.at[1], back_recv.at[1]))

    for shift in SHIFTS:
        there = shifted(*shift)
        for to_core, (source, target, send_sem, recv_sem) in enumerate(sides):
            pltpu.make_async_remote_copy(
                src_ref=source.at[chip_index(*there)],
                dst_ref=target.at[mine],
                send_sem=send_sem,
                recv_sem=recv_sem,
                device_id=device(*there, to_core),
                device_id_type=MESH,
            ).start()

    def end(own):
        source, target, send_sem, recv_sem = sides[own]
        other_source, other_target, other_send, other_recv = sides[1 - own]
        groups = 4 - own
        pltpu.make_async_remote_copy(
            src_ref=other_source.at[me],
            dst_ref=other_target.at[mine],
            send_sem=other_send,
            recv_sem=other_recv,
            device_id=sibling,
            device_id_type=MESH,
        ).start()
        keep_back = pltpu.make_async_copy(source.at[me], target.at[mine], local)
        keep_back.start()
        keep_back.wait()

        def whole(refs, sems, n):
            return pltpu.make_async_remote_copy(
                src_ref=refs[0].at[pl.ds(0, n)],
                dst_ref=refs[1].at[pl.ds(0, n)],
                send_sem=sems[0],
                recv_sem=sems[1],
                device_id=sibling,
                device_id_type=MESH,
            )

        whole((target, target), (send_sem, recv_sem), 2 * CHIPS - 1).wait_recv()

        def total(ch, carry):
            return carry + target[ch].astype(F32)

        none = jnp.zeros((groups * 8, 128), F32)
        middle = lax.fori_loop(0, 32, total, none, unroll=16) * (1 / 32)

        def spread(ch, sums):
            centred = target[ch].astype(F32) - middle
            return sums[0] + centred, sums[1] + centred * centred

        moved_by, var = lax.fori_loop(0, 128, spread, (none, none), unroll=16)
        moved_by = moved_by * (1 / 128)
        mean = middle + moved_by
        var = jnp.maximum(var * (1 / 128) - moved_by * moved_by, 0.0)
        scale = lax.rsqrt(var + 1e-05)

        def normalise(ch, carry):
            finished[pl.ds(pl.multiple_of(ch * BACK, BACK), groups * 8), :] = (target[ch].astype(F32) - mean) * scale
            return carry

        lax.fori_loop(0, 128, normalise, 0, unroll=16)

        def projected(row, n_blocks):
            values = finished[pl.ds(row, 128, stride=BACK), :]
            got = lax.dot_general(values.astype(BF16), scaled, (((0,), (0,)), ((), ())), preferred_element_type=F32)
            return got[: 16 * n_blocks] + offset

        def put(got, inner, p, s):
            at = p // 5 * 8 + inner
            for h in range(2):
                cols = pl.ds(h * 40 + p % 5 * 8, 8)
                rows = got[s * 16 + h * 8 : s * 16 + h * 8 + 8, :]
                out[at, cols, :] = (rows * gating[at, cols, :]).astype(BF16)

        passed = pltpu.make_async_remote_copy(
            src_ref=last_out,
            dst_ref=last_in,
            send_sem=last_send,
            recv_sem=last_recv,
            device_id=sibling,
            device_id_type=MESH,
        )
        if own == 0:

            def last_row(inner, carry):
                got = projected(24 + inner, 2)
                put(got, inner, 24, 0)
                last_out[inner] = (got[16:32, :] * last_gating[inner]).astype(BF16)
                return carry

            lax.fori_loop(0, 8, last_row, 0, unroll=8)
            passed.start()

        def finish(inner, carry):
            for g in range(3):
                got = projected(g * 8 + inner, 8)
                for s in range(8):
                    put(got, inner, 8 * g + s, s)
            return carry

        lax.fori_loop(0, 8, finish, 0, unroll=8)
        if own == 0:
            passed.wait_send()
        else:
            passed.wait_recv()
            for inner in range(8):
                for h in range(2):
                    out[32 + inner, pl.ds(h * 40 + 32, 8), :] = last_in[inner, h * 8 : h * 8 + 8, :]
        whole((source, source), (send_sem, recv_sem), CHIPS - 1).wait_send()
        whole((other_source, other_source), (other_send, other_recv), CHIPS).wait_send()

    pl.when(core == 0)(functools.partial(end, 0))
    pl.when(core == 1)(functools.partial(end, 1))
    pltpu.make_async_remote_copy(
        src_ref=packed.at[pl.ds(0, CHIPS - 1)],
        dst_ref=arrived.at[pl.ds(0, CHIPS - 1)],
        send_sem=send,
        recv_sem=recv.at[0],
        device_id=sibling,
        device_id_type=MESH,
    ).wait_send()


def body(*args):
    pair, mask, norm_gain, norm_bias, proj_w, gate_w, out_gain, out_bias, out_w, out_gate_w = args
    operands = (
        pair, mask, norm_gain.reshape(1, 128), norm_bias.reshape(1, 128), proj_w, gate_w,
        out_gain.reshape(1, 128), out_bias.reshape(1, 128), out_w, out_gate_w,
    )
    dma = pltpu.SemaphoreType.DMA
    return pl.pallas_call(
        kernel,
        out_shape=pltpu.VMEM(pair.shape, BF16),
        in_specs=[pl.BlockSpec(memory_space=pl.ANY)] * 10,
        out_specs=pl.BlockSpec(memory_space=pltpu.VMEM),
        scratch_shapes=[pltpu.VMEM(a.shape, a.dtype) for a in operands]
        + [
            dma((10,)),
            pltpu.VMEM((2, 40, 80, 128), BF16),
            pltpu.VMEM((2, 32, 128), F32),
            pltpu.VMEM((40, 80, 128), F32),
            pltpu.VMEM((256, 128), BF16),
            pltpu.VMEM((CHIPS * ROWS + ROWS, 128), F32),
            pltpu.VMEM((CHIPS, ROWS, 128), BF16),
            pltpu.VMEM((CHIPS, ROWS, 128), BF16),
            pltpu.VMEM((640, 640), BF16),
            pltpu.VMEM((640, 640), BF16),
            pltpu.VMEM((1024, 1024), BF16),
            pltpu.VMEM((640, 640), BF16),
            pltpu.VMEM((CHIPS, BACK, 128), BF16),
            pltpu.VMEM((CHIPS, BACK - 8, 128), BF16),
            pltpu.VMEM((2 * CHIPS, BACK, 128), BF16),
            pltpu.VMEM((2 * CHIPS, BACK - 8, 128), BF16),
            pltpu.VMEM((8, 16, 128), BF16),
            pltpu.VMEM((8, 16, 128), BF16),
            pltpu.VMEM((8, 16, 128), F32),
            pltpu.VMEM((128 * BACK + BACK, 128), F32),
            dma((3,)), dma((3,)), dma, dma((4,)), dma((2,)), dma((2,)), dma, dma, dma, pltpu.SemaphoreType.REGULAR, pltpu.SemaphoreType.REGULAR,
        ],
        compiler_params=pltpu.CompilerParams(
            collective_id=0, has_side_effects=True, vmem_limit_bytes=56 * 2**20
        ),
    )(*operands)


def solution(mesh):
    placed = (P("row", "col", None), P("row", "col"), P(), P(), P(), P(), P(), P(), P(), P())
    return jax.shard_map(body, mesh=mesh, in_specs=placed, out_specs=P("row", "col", None), check_vma=False)
```

```python
import functools

import jax
import jax.numpy as jnp
from jax import lax
from jax.experimental import pallas as pl
from jax.experimental.pallas import tpu as pltpu
from jax.sharding import PartitionSpec as P

MESH = pl.DeviceIdType.MESH
F32, BF16 = jnp.float32, jnp.bfloat16
NT = (((1,), (1,)), ((), ()))
CHIPS = 64
ROWS = 104
BACK = 32


def device(x, y, z, core):
    return (y * 4 + (z // 2) * 2 + core, x * 2 + z % 2)


def chip_index(x, y, z):
    return (y * 2 + z // 2) * 8 + x * 2 + z % 2


def channel_of(x, y, z):
    return x * 16 + y * 4 + z


def distance(shift):
    return sum(min(d, 4 - d) for d in shift)


SHIFTS = sorted(
    [(n // 16, n // 4 % 4, n % 4) for n in range(1, CHIPS)],
    key=lambda s: (-max(distance(s), 2), -min(s[1], 4 - s[1]), -distance(s), (s[0] * 7 + s[1] * 11 + s[2] * 13) % 16),
)


def kernel(
    pair_in, mask_in, norm_gain_in, norm_bias_in, proj_w_in, gate_w_in, out_gain_in, out_bias_in, out_w_in, out_gate_w_in,
    out,
    pair, mask, norm_gain, norm_bias, proj_w, gate_w, out_gain, out_bias, out_w, out_gate_w, load,
    normed, masks, gating, weights, wide, packed, arrived, left, right, swap, combined, back_0, back_1,
    returned_0, returned_1, last_out, last_in, last_gating, finished,
    sibling_send, sibling_recv, send, recv, back_send, back_recv, last_send, last_recv, local, entered_y, entered_z,
):
    r, c = lax.axis_index("row"), lax.axis_index("col")
    x, y, z, core = c // 2, r // 4, ((r // 2) % 2) * 2 + c % 2, r % 2
    me, channel = chip_index(x, y, z), channel_of(x, y, z)

    def shifted(dx, dy, dz):
        return (x + dx) % 4, (y + dy) % 4, (z + dz) % 4

    barrier = pltpu.get_barrier_semaphore()
    sibling = device(x, y, z, 1 - core)
    along = [[device(*shifted(*(d * (a == n) for a in range(3))), core) for d in (1, 2, 3)] for n in range(3)]
    for there in [sibling] + along[0] + along[1] + along[2]:
        pl.semaphore_signal(barrier, inc=1, device_id=there, device_id_type=MESH)

    def pass_on(sem, line):
        for there in line:
            pl.semaphore_signal(sem, inc=1, device_id=there, device_id_type=MESH)

    sources = (
        pair_in, mask_in, norm_gain_in, norm_bias_in, proj_w_in, gate_w_in, out_gain_in, out_bias_in, out_w_in, out_gate_w_in
    )
    places = (pair, mask, norm_gain, norm_bias, proj_w, gate_w, out_gain, out_bias, out_w, out_gate_w)
    loads = [pltpu.make_async_copy(a, b, load.at[n]) for n, (a, b) in enumerate(zip(sources, places))]
    for n in (1, 0, 2, 3, 4, 5, 6, 7, 8, 9):
        loads[n].start()
    loads[1].wait()

    lane = lax.broadcasted_iota(jnp.int32, (8, 128), 1)
    finished[0:40, 0:128] = jnp.zeros((40, 128), F32)
    finished[0:40, 0:80] = mask[...].astype(F32)
    for g in range(3):
        valid = jnp.zeros((8, 128), F32)
        for s in range(8):
            p = 8 * g + s
            turned = pltpu.roll(finished[p // 5 * 8 : p // 5 * 8 + 8, :], (s - p % 5) * 16 % 128, 1)
            valid = jnp.where(lane // 16 == s, turned, valid)
        masks[core, g * 8 : g * 8 + 8, :] = valid
    last = jnp.zeros((8, 128), F32)
    for n in range(8):
        turned = pltpu.roll(jnp.broadcast_to(finished[32 + n : 33 + n, :], (8, 128)), (n - 4) * 16 % 128, 1)
        last = jnp.where(lane // 16 == n, turned, last)
    masks[core, 24:32, :] = last

    for n in (0, 2, 3):
        loads[n].wait()
    gain, bias = norm_gain[...], norm_bias[...]

    def norm_rows(n, carry):
        values = pair[pl.ds(n * 4, 4)].astype(F32)
        mean = jnp.mean(values, axis=-1, keepdims=True)
        centred = values - mean
        var = jnp.mean(centred * centred, axis=-1, keepdims=True)
        normed[core, pl.ds(n * 4, 4)] = (centred * lax.rsqrt(var + 1e-05) * gain + bias).astype(BF16)
        return carry

    def to_sibling(ref, send_sem, recv_sem):
        return pltpu.make_async_remote_copy(
            src_ref=ref, dst_ref=ref, send_sem=send_sem, recv_sem=recv_sem, device_id=sibling, device_id_type=MESH
        )

    exchange = [
        to_sibling(masks.at[core], sibling_send.at[0], sibling_recv.at[0]),
        to_sibling(normed.at[core, pl.ds(0, 20)], sibling_send.at[1], sibling_recv.at[1]),
        to_sibling(normed.at[core, pl.ds(20, 20)], sibling_send.at[2], sibling_recv.at[2]),
    ]
    lax.fori_loop(0, 5, norm_rows, 0, unroll=5)
    pl.semaphore_wait(barrier, 10)
    exchange[0].start()
    exchange[1].start()
    pass_on(entered_y, along[0] + along[1] + along[2])
    lax.fori_loop(5, 10, norm_rows, 0, unroll=5)
    exchange[2].start()

    for n in (4, 5, 6, 7, 8, 9):
        loads[n].wait()
    half = pl.ds(pl.multiple_of(core * 64, 64), 64)
    for n, w in enumerate((proj_w, gate_w)):
        for side in range(2):
            finished[0:128, :] = jnp.transpose(w[:, side * 128 : side * 128 + 128].astype(F32))
            weights[(n * 2 + side) * 64 : (n * 2 + side) * 64 + 64, :] = finished[half, :].astype(BF16)

    def project(who):
        def values_of(tokens, valid):
            got = lax.dot_general(weights[...], tokens, NT, preferred_element_type=F32)
            return got[:128] * (0.5 * jnp.tanh(0.5 * got[128:]) + 0.5) * valid

        def put(values, row, side_rows):
            for side in range(2):
                wide[pl.ds(side * side_rows + row, CHIPS, stride=ROWS), :] = values[side * 64 : side * 64 + 64]

        def project_row(inner, carry):
            tokens = [
                normed[who, (p // 5) * 8 + inner, (p % 5) * 16 : (p % 5) * 16 + 16, :] for p in range(24)
            ]
            valid = jnp.concatenate([masks[who, pl.ds(g * 8 + inner, 1), :] for g in range(3)], axis=1)
            values = values_of(jnp.concatenate(tokens, axis=0), valid)
            for g in range(3):
                put(values[:, g * 128 : g * 128 + 128], g * 16 + who * 8 + inner, 48)
            return carry

        lax.fori_loop(0, 8, project_row, 0, unroll=8)
        last_tokens = [normed[who, 32 + n, 64:80, :] for n in range(8)]
        put(values_of(jnp.concatenate(last_tokens, axis=0), masks[who, 24:25, :]), 96 + who, 2)

    for row in range(100, ROWS):
        wide[pl.ds(row, CHIPS, stride=ROWS), :] = jnp.zeros((CHIPS, 128), F32)
    project(core)
    pl.semaphore_wait(entered_y, 9)
    pass_on(entered_z, along[2])
    for e in exchange:
        e.wait()
    project(1 - core)

    def narrow(m, carry):
        packed[m] = wide[pl.ds(pl.multiple_of(m * ROWS, 8), ROWS), :].astype(BF16)
        return carry

    lax.fori_loop(0, CHIPS, narrow, 0, unroll=4)

    def post(shifts):
        for shift in shifts:
            there = shifted(*shift)
            pltpu.make_async_remote_copy(
                src_ref=packed.at[channel_of(*there)],
                dst_ref=arrived.at[me],
                send_sem=send,
                recv_sem=recv.at[shift[1]],
                device_id=device(*there, core),
                device_id_type=MESH,
            ).start()

    early = [s for s in SHIFTS if 0 in s and distance(s) > 2]
    post(early)
    pl.semaphore_wait(entered_z, 3)
    post([s for s in SHIFTS if s not in early])
    keep = pltpu.make_async_copy(packed.at[channel], arrived.at[me], local)
    keep.start()

    def gate_row(i, carry):
        gate = jnp.dot(normed[core, i], out_gate_w[...], preferred_element_type=F32)
        gating[i] = 0.5 * jnp.tanh(0.5 * gate) + 0.5
        return carry

    lax.fori_loop(0, 40, gate_row, 0)
    for inner in range(8):
        tokens = jnp.concatenate([normed[1, 32 + inner, h * 40 + 32 : h * 40 + 40, :] for h in range(2)], axis=0)
        gate = jnp.dot(tokens, out_gate_w[...], preferred_element_type=F32)
        last_gating[inner] = 0.5 * jnp.tanh(0.5 * gate) + 0.5
    for a in range(8):
        at = lax.broadcasted_iota(jnp.int32, (128, 1024), 0)
        to = lax.broadcasted_iota(jnp.int32, (128, 1024), 1)
        swap[a * 128 : a * 128 + 128, :] = (to == (at // 16) * 128 + a * 16 + at % 16).astype(F32).astype(BF16)
    w_t = jnp.transpose(out_w[...].astype(F32))
    offset = lax.dot_general(out_bias[...], w_t, NT, preferred_element_type=F32, precision=lax.Precision.HIGHEST)
    scaled = jnp.transpose(w_t * out_gain[...]).astype(BF16)

    for dy in (2, 1, 3, 0):
        n_from = 16 if dy else 15
        pltpu.make_async_remote_copy(
            src_ref=packed.at[pl.ds(0, n_from)],
            dst_ref=arrived.at[pl.ds(0, n_from)],
            send_sem=send,
            recv_sem=recv.at[dy],
            device_id=sibling,
            device_id_type=MESH,
        ).wait_recv()
        if dy == 0:
            keep.wait()
        first = (y + 4 - dy) % 4 * 2
        beside = [
            jnp.concatenate([arrived[(first + m) * 8 + k] for m in range(2)], axis=0) for k in range(8)
        ]
        moved = jnp.dot(jnp.concatenate(beside, axis=1), swap[...], preferred_element_type=F32)
        for m in range(2):
            for side, target in enumerate((left, right)):
                for p in range(24):
                    row, col = m * ROWS + side * 48 + p // 8 * 16, p % 8 * 128
                    at = pl.ds(pl.multiple_of(p // 5 * 128 + (first + m) * 16, 16), 16)
                    target[at, p % 5 * 128 : p % 5 * 128 + 128] = moved[row : row + 16, col : col + 128].astype(BF16)
                for n in range(16):
                    row = m * ROWS + 96 + side * 2 + n // 8
                    finished[n : n + 1, :] = moved[row : row + 1, n % 8 * 128 : n % 8 * 128 + 128]
                at = pl.ds(pl.multiple_of(512 + (first + m) * 16, 16), 16)
                target[at, 512:640] = finished[0:16, :].astype(BF16)

    got = lax.dot_general(left[...], right[...], NT, preferred_element_type=F32)
    combined[...] = got.astype(BF16)
    turned = [got[512 + m * 16 + h : 512 + m * 16 + h + 8, 512:640] for m in range(8) for h in (8, 0)]
    last_turned = jnp.concatenate(turned, axis=0).astype(BF16)

    def block(p):
        return combined[p // 5 * 128 : p // 5 * 128 + 128, p % 5 * 128 : p % 5 * 128 + 128]

    groups = [jnp.concatenate([block(p) for p in range(8 * g, 8 * g + 8)], axis=1) for g in range(3)]
    moved_3 = jnp.dot(jnp.concatenate(groups, axis=0), swap[...], preferred_element_type=F32)
    last = jnp.concatenate([block(24), last_turned], axis=1)
    moved = [moved_3[g * 128 : g * 128 + 128] for g in range(3)]
    moved.append(jnp.dot(last, swap[0:256, :], preferred_element_type=F32))
    for m in range(8):
        for k in range(8):
            for h, (target, groups) in enumerate(((back_0, 4), (back_1, 3))):
                row = m * 16 + h * 8
                tiles = [v[row : row + 8, k * 128 : k * 128 + 128] for v in moved[:groups]]
                target[m * 8 + k] = jnp.concatenate(tiles, axis=0).astype(BF16)

    mine = core * CHIPS + channel
    sides = ((back_0, returned_0, back_send.at[0], back_recv.at[0]), (back_1, returned_1, back_send.at[1], back_recv.at[1]))

    for shift in sorted(SHIFTS, key=lambda s: (-distance(s), (s[0] * 7 + s[1] * 11 + s[2] * 13) % 16)):
        there = shifted(*shift)
        for to_core, (source, target, send_sem, recv_sem) in enumerate(sides):
            pltpu.make_async_remote_copy(
                src_ref=source.at[chip_index(*there)],
                dst_ref=target.at[mine],
                send_sem=send_sem,
                recv_sem=recv_sem,
                device_id=device(*there, to_core),
                device_id_type=MESH,
            ).start()

    def end(own):
        source, target, send_sem, recv_sem = sides[own]
        other_source, other_target, other_send, other_recv = sides[1 - own]
        groups = 4 - own
        pltpu.make_async_remote_copy(
            src_ref=other_source.at[me],
            dst_ref=other_target.at[mine],
            send_sem=other_send,
            recv_sem=other_recv,
            device_id=sibling,
            device_id_type=MESH,
        ).start()
        keep_back = pltpu.make_async_copy(source.at[me], target.at[mine], local)
        keep_back.start()
        keep_back.wait()

        def whole(refs, sems, n):
            return pltpu.make_async_remote_copy(
                src_ref=refs[0].at[pl.ds(0, n)],
                dst_ref=refs[1].at[pl.ds(0, n)],
                send_sem=sems[0],
                recv_sem=sems[1],
                device_id=sibling,
                device_id_type=MESH,
            )

        whole((target, target), (send_sem, recv_sem), 2 * CHIPS - 1).wait_recv()

        def total(ch, carry):
            return carry + target[ch].astype(F32)

        none = jnp.zeros((groups * 8, 128), F32)
        middle = lax.fori_loop(0, 32, total, none, unroll=16) * (1 / 32)

        def spread(ch, sums):
            centred = target[ch].astype(F32) - middle
            return sums[0] + centred, sums[1] + centred * centred

        moved_by, var = lax.fori_loop(0, 128, spread, (none, none), unroll=16)
        moved_by = moved_by * (1 / 128)
        mean = middle + moved_by
        var = jnp.maximum(var * (1 / 128) - moved_by * moved_by, 0.0)
        scale = lax.rsqrt(var + 1e-05)

        def normalise(ch, carry):
            finished[pl.ds(pl.multiple_of(ch * BACK, BACK), groups * 8), :] = (target[ch].astype(F32) - mean) * scale
            return carry

        lax.fori_loop(0, 128, normalise, 0, unroll=16)

        def projected(row, n_blocks):
            values = finished[pl.ds(row, 128, stride=BACK), :]
            got = lax.dot_general(values.astype(BF16), scaled, (((0,), (0,)), ((), ())), preferred_element_type=F32)
            return got[: 16 * n_blocks] + offset

        def put(got, inner, p, s):
            at = p // 5 * 8 + inner
            for h in range(2):
                cols = pl.ds(h * 40 + p % 5 * 8, 8)
                rows = got[s * 16 + h * 8 : s * 16 + h * 8 + 8, :]
                out[at, cols, :] = (rows * gating[at, cols, :]).astype(BF16)

        passed = pltpu.make_async_remote_copy(
            src_ref=last_out,
            dst_ref=last_in,
            send_sem=last_send,
            recv_sem=last_recv,
            device_id=sibling,
            device_id_type=MESH,
        )
        if own == 0:

            def last_row(inner, carry):
                got = projected(24 + inner, 2)
                put(got, inner, 24, 0)
                last_out[inner] = (got[16:32, :] * last_gating[inner]).astype(BF16)
                return carry

            lax.fori_loop(0, 8, last_row, 0, unroll=8)
            passed.start()

        def finish(inner, carry):
            for g in range(3):
                got = projected(g * 8 + inner, 8)
                for s in range(8):
                    put(got, inner, 8 * g + s, s)
            return carry

        lax.fori_loop(0, 8, finish, 0, unroll=8)
        if own == 0:
            passed.wait_send()
        else:
            passed.wait_recv()
            for inner in range(8):
                for h in range(2):
                    out[32 + inner, pl.ds(h * 40 + 32, 8), :] = last_in[inner, h * 8 : h * 8 + 8, :]
        whole((source, source), (send_sem, recv_sem), CHIPS - 1).wait_send()
        whole((other_source, other_source), (other_send, other_recv), CHIPS).wait_send()

    pl.when(core == 0)(functools.partial(end, 0))
    pl.when(core == 1)(functools.partial(end, 1))
    pltpu.make_async_remote_copy(
        src_ref=packed.at[pl.ds(0, CHIPS - 1)],
        dst_ref=arrived.at[pl.ds(0, CHIPS - 1)],
        send_sem=send,
        recv_sem=recv.at[0],
        device_id=sibling,
        device_id_type=MESH,
    ).wait_send()


def body(*args):
    pair, mask, norm_gain, norm_bias, proj_w, gate_w, out_gain, out_bias, out_w, out_gate_w = args
    operands = (
        pair, mask, norm_gain.reshape(1, 128), norm_bias.reshape(1, 128), proj_w, gate_w,
        out_gain.reshape(1, 128), out_bias.reshape(1, 128), out_w, out_gate_w,
    )
    dma = pltpu.SemaphoreType.DMA
    return pl.pallas_call(
        kernel,
        out_shape=pltpu.VMEM(pair.shape, BF16),
        in_specs=[pl.BlockSpec(memory_space=pl.ANY)] * 10,
        out_specs=pl.BlockSpec(memory_space=pltpu.VMEM),
        scratch_shapes=[pltpu.VMEM(a.shape, a.dtype) for a in operands]
        + [
            dma((10,)),
            pltpu.VMEM((2, 40, 80, 128), BF16),
            pltpu.VMEM((2, 32, 128), F32),
            pltpu.VMEM((40, 80, 128), F32),
            pltpu.VMEM((256, 128), BF16),
            pltpu.VMEM((CHIPS * ROWS + ROWS, 128), F32),
            pltpu.VMEM((CHIPS, ROWS, 128), BF16),
            pltpu.VMEM((CHIPS, ROWS, 128), BF16),
            pltpu.VMEM((640, 640), BF16),
            pltpu.VMEM((640, 640), BF16),
            pltpu.VMEM((1024, 1024), BF16),
            pltpu.VMEM((640, 640), BF16),
            pltpu.VMEM((CHIPS, BACK, 128), BF16),
            pltpu.VMEM((CHIPS, BACK - 8, 128), BF16),
            pltpu.VMEM((2 * CHIPS, BACK, 128), BF16),
            pltpu.VMEM((2 * CHIPS, BACK - 8, 128), BF16),
            pltpu.VMEM((8, 16, 128), BF16),
            pltpu.VMEM((8, 16, 128), BF16),
            pltpu.VMEM((8, 16, 128), F32),
            pltpu.VMEM((128 * BACK + BACK, 128), F32),
            dma((3,)), dma((3,)), dma, dma((4,)), dma((2,)), dma((2,)), dma, dma, dma, pltpu.SemaphoreType.REGULAR, pltpu.SemaphoreType.REGULAR,
        ],
        compiler_params=pltpu.CompilerParams(
            collective_id=0, has_side_effects=True, vmem_limit_bytes=56 * 2**20
        ),
    )(*operands)


def solution(mesh):
    placed = (P("row", "col", None), P("row", "col"), P(), P(), P(), P(), P(), P(), P(), P())
    return jax.shard_map(body, mesh=mesh, in_specs=placed, out_specs=P("row", "col", None), check_vma=False)
```
